256 devices in a mesh: ang: 16 (over y, x_lo, core), row: 16 (over z, x_hi).
Axes of the slice: x: 4 (x_hi: 2, x_lo: 2; x = x_hi * 2 + x_lo), y: 4, z: 8, core: 2. Of those that a mesh axis runs over, the one named last changes fastest.
Arguments:
- projections: float32 [256, 256, 4608], P('ang', 'row'), may hold values from -6 to 6
- phase_kernel: float32 [5, 5], replicated, may hold values from -1 to 1
- correlation: int32 [1], replicated, may hold values from 1472 to 1919
- offset: int32 [1], replicated, may hold values from 0 to 448
Outputs:
- sinograms: float32 [256, 128, 8192], P(('row', 'ang'))
The draws below stay inside these ranges and needn't reach their ends.
All inputs are finite; a program needn't handle non-finite values.
Results may differ from the reference program's by a relative error of at most 0.000076.
Values sent between devices are 32-bit elements; how exact they have to be, the bound alone decides.
No kernel may reach another device: no remote copies, remote signals or barrier semaphores. Data moves between devices by JAX's collectives and lax.ppermute only.
A program may use at most 128 MiB of HBM per device.

```python
import jax
import jax.numpy as jnp
from jax import lax

W = 4608
S = 8192
ANG = 256
ROWS = 256


def level_of(own_key, extent, pieces, low, high):
    gain, own = 1.0, jax.random.fold_in(own_key, 6)
    for axis_at, shards_of in pieces:
        steps = jnp.exp(jax.random.uniform(jax.random.fold_in(own, axis_at), (shards_of,), jnp.float32, low / len(pieces), high / len(pieces)))
        gain = gain * jnp.repeat(steps, extent[axis_at] // shards_of).reshape([-1 if axis == axis_at else 1 for axis in range(len(extent))])
    return gain


def centred(key, dims, scale, most, pieces=(), kind=jnp.bfloat16):
    values = scale * jax.random.normal(key, dims, jnp.float32)
    if pieces:
        values = values * level_of(key, dims, pieces, -0.22, 0.18)
    return jnp.clip(values, -most, most).astype(kind)


def setup_inputs(seed: int = 0) -> dict:
    arg_keys = jax.random.split(jax.random.key(seed), 5)
    return {
        "projections": centred(arg_keys[0], (ANG, ROWS, W), 1.0, 6.0, ((0, 16), (1, 16)), jnp.float32),
        "phase_kernel": centred(arg_keys[1], (5, 5), 0.2, 1.0, (), jnp.float32),
        "correlation": jax.random.randint(arg_keys[2], (1,), 2 * W - S + (S - W) // 8, 2 * W - S + (S - W) // 4).astype(jnp.int32),
        "offset": jax.random.randint(arg_keys[3], (1,), 0, (S - W) // 8 + 1).astype(jnp.int32),
    }


def phase_filter(projections, phase_kernel):
    padded = jnp.pad(projections, ((0, 0), (2, 2), (2, 2)))
    rows_here = projections.shape[1]
    columns = projections.shape[2]
    result = jnp.zeros(projections.shape, jnp.float32)
    for row_step in range(5):
        for col_step in range(5):
            result = result + phase_kernel[row_step, col_step] * padded[:, row_step:row_step + rows_here, col_step:col_step + columns]
    return result


def stitch(own_part, opposite_part, correlation_cols, offset_cols):
    columns = own_part.shape[-1]
    last_axis = own_part.ndim - 1
    left_edge = offset_cols + columns - correlation_cols
    pad_config = [(0, 0)] * last_axis + [(S, S)]
    own_full = lax.dynamic_slice_in_dim(jnp.pad(own_part, pad_config), (S - left_edge).astype(jnp.int32), S, axis=last_axis)
    reversed_part = jnp.flip(opposite_part, axis=last_axis)
    opposite_full = lax.dynamic_slice_in_dim(jnp.pad(reversed_part, pad_config), (S - offset_cols).astype(jnp.int32), S, axis=last_axis)
    stitched_cols = jnp.arange(S, dtype=jnp.int32)
    blend = ((stitched_cols - left_edge).astype(jnp.float32) + 0.5) / correlation_cols.astype(jnp.float32)
    inside = stitched_cols < left_edge + correlation_cols
    before = stitched_cols < left_edge
    own_weight = jnp.where(before, 0.0, jnp.where(inside, blend, 1.0)).astype(jnp.float32)
    opposite_weight = jnp.where(before, 1.0, jnp.where(inside, 1.0 - blend, 0.0)).astype(jnp.float32)
    return own_weight * own_full + opposite_weight * opposite_full


def reference(projections, phase_kernel, correlation, offset):
    filtered = phase_filter(projections, phase_kernel)
    correlation_cols = correlation[0]
    offset_cols = offset[0]
    pairs = ANG // 2
    frequency = jnp.arange(S // 2 + 1, dtype=jnp.float32)
    ramp_gain = 2.0 * frequency / S

    def one_row(row_index):
        sheet = lax.dynamic_index_in_dim(filtered, row_index, 1, keepdims=False)
        stitched = stitch(sheet[:pairs], sheet[pairs:], correlation_cols, offset_cols)
        spectrum = jnp.fft.rfft(stitched, axis=-1)
        return jnp.fft.irfft(spectrum * ramp_gain, n=S, axis=-1).astype(jnp.float32)

    return lax.map(one_row, jnp.arange(ROWS, dtype=jnp.int32))
```

```python
import functools
import math

import jax
import jax.numpy as jnp
import numpy as np
from jax import lax
from jax.experimental import pallas as pl
from jax.experimental.pallas import tpu as pltpu
from jax.sharding import PartitionSpec as P

W = 4608
S = 8192
LANES = 128
SUB = 8
WT = W // LANES
ST = S // LANES
CT = 61
VMEM_LIMIT = 48 * 1024 * 1024

f32 = jnp.float32
bf16 = jnp.bfloat16


def tables():
    k1 = np.arange(64)
    n2 = np.arange(128)
    turn = 2 * np.pi * (k1[:, None] * n2[None, :]) / S
    twiddle = np.stack([np.cos(turn), -np.sin(turn)])
    twiddle = np.repeat(twiddle[:, :, None, :], SUB, axis=2).astype(np.float32)
    freq = k1[:, None] + 64 * n2[None, :]
    gain = 2.0 * np.minimum(freq, S - freq) / S / S
    gain = np.repeat(gain[:, None, :], SUB, axis=1).reshape(64 * SUB, 128).astype(np.float32)
    angle = 2 * np.pi * ((n2[:, None] * n2[None, :]) % 128) / 128
    c, s = np.cos(angle), np.sin(angle)
    forward = np.block([[c, -s], [s, c]]).astype(np.float32)
    return twiddle, gain, forward


def split(matrix):
    high = matrix.astype(jnp.bfloat16)
    low = (matrix - high.astype(np.float32)).astype(jnp.bfloat16)
    return high, low


def cadd(a, b):
    return (a[0] + b[0], a[1] + b[1])


def csub(a, b):
    return (a[0] - b[0], a[1] - b[1])


def turn_quarter(a, sign):
    return (-a[1], a[0]) if sign > 0 else (a[1], -a[0])


def dft4(x0, x1, x2, x3, sign):
    a0, a1 = cadd(x0, x2), csub(x0, x2)
    a2, a3 = cadd(x1, x3), turn_quarter(csub(x1, x3), sign)
    return cadd(a0, a2), cadd(a1, a3), csub(a0, a2), csub(a1, a3)


def dft8(x, sign):
    e = dft4(x[0], x[2], x[4], x[6], sign)
    o = dft4(x[1], x[3], x[5], x[7], sign)
    h = math.sqrt(0.5)
    r, m = o[1]
    o1 = ((r - m) * h, (m + r) * h) if sign > 0 else ((r + m) * h, (m - r) * h)
    o2 = turn_quarter(o[2], sign)
    r, m = o[3]
    o3 = ((r + m) * -h, (r - m) * h) if sign > 0 else ((m - r) * h, (r + m) * -h)
    odd = (o[0], o1, o2, o3)
    return [cadd(e[k], odd[k]) for k in range(4)] + [csub(e[k], odd[k]) for k in range(4)]


def const_turn(a, count, sign):
    count %= 64
    if count == 0:
        return a
    c = math.cos(2 * math.pi * count / 64)
    s = sign * math.sin(2 * math.pi * count / 64)
    return (a[0] * c - a[1] * s, a[0] * s + a[1] * c)


def lane_index():
    return lax.broadcasted_iota(jnp.int32, (SUB, LANES), 1)


def gather_rows(x_hbm, first, up_ref, dn_ref, flat, sems, xs):
    copies = [
        pltpu.make_async_copy(
            x_hbm.at[pl.ds(first, 16 * SUB), t * LANES : (t + 1) * LANES], flat.at[t], sems.at[t]
        )
        for t in range(WT)
    ]
    for copy in copies:
        copy.start()
    for r in range(2):
        for t in range(WT):
            cols = slice(t * LANES, (t + 1) * LANES)
            xs[r, t] = up_ref[r, :, cols]
            xs[18 + r, t] = dn_ref[r, :, cols]

    for copy in copies:
        copy.wait()

    @pl.loop(0, 16)
    def _(r):
        for t in range(WT):
            xs[r + 2, t] = flat[t, pl.ds(r, SUB, stride=16), :]


def filter_row(taps, w_ref, xs, r, store):
    lane = lane_index()
    zero = jnp.zeros((SUB, LANES), f32)
    r0, r1, left, right3, right4 = zero, zero, None, None, None
    for t in range(WT + 1):
        if t < WT:
            rows = [xs[r + i, t] for i in range(5)]
            acc = []
            for j in range(5):
                total = taps[j] * rows[0]
                for i in range(1, 5):
                    total = total + taps[5 * i + j] * rows[i]
                acc.append(total)
            n0, n1 = pltpu.roll(acc[0], 2, 1), pltpu.roll(acc[1], 1, 1)
            n3, n4 = pltpu.roll(acc[3], LANES - 1, 1), pltpu.roll(acc[4], LANES - 2, 1)
        else:
            n3 = n4 = zero
        if t > 0:
            value = left + jnp.where(lane < LANES - 1, right3, n3) + jnp.where(lane < LANES - 2, right4, n4)
            store(t - 1, value * w_ref[t - 1])
        if t < WT:
            left = acc[2] + jnp.where(lane >= 2, n0, r0) + jnp.where(lane >= 1, n1, r1)
            r0, r1, right3, right4 = n0, n1, n3, n4


def stitch(own, opp, put, add, shift):
    lane = lane_index()
    backwards = LANES - 1 - lane
    zero = jnp.zeros((SUB, LANES), f32)
    for t in range(CT):
        put(t, jnp.take_along_axis(opp(WT - 1 - t), backwards, axis=1) if t < WT else zero)
    whole, part = shift // LANES, lax.rem(shift, LANES)
    before = zero
    for t in range(WT + 1):
        now = pltpu.roll(own(t), part, 1) if t < WT else zero
        add(whole + t, jnp.where(lane >= part, now, before))
        before = now


def place(source, sig, side, shift):
    lane = lane_index()
    zero = jnp.zeros((SUB, LANES), f32)
    whole, part = shift // LANES, lax.rem(shift, LANES)
    for t in range(4):
        sig[side, t] = zero
        sig[side, ST - 4 + t] = zero
    before = zero
    for t in range(CT + 1):
        now = pltpu.roll(source(t), part, 1) if t < CT else zero
        sig[side, whole + t] = jnp.where(lane >= part, now, before)
        before = now


def matmul3(x, high, low):
    xh = x.astype(bf16)
    xl = (x - xh.astype(f32)).astype(bf16)
    dot = functools.partial(jnp.dot, preferred_element_type=f32)
    return dot(xh, low) + dot(xl, high) + dot(xh, high)


def ramp(sig, mid, spec, tw_ref, gain_ref, fh, fl, gh, gl, put):
    for b in range(8):
        x = dft8([(sig[0, 8 * a + b], sig[1, 8 * a + b]) for a in range(8)], -1)
        for c in range(8):
            mid[0, 8 * b + c], mid[1, 8 * b + c] = const_turn(x[c], b * c, -1)
    for c in range(8):
        y = dft8([(mid[0, 8 * b + c], mid[1, 8 * b + c]) for b in range(8)], -1)
        for d in range(8):
            k = c + 8 * d
            tr, ti = tw_ref[0, k], tw_ref[1, k]
            re, im = y[d]
            spec[k * SUB : (k + 1) * SUB, :LANES] = re * tr - im * ti
            spec[k * SUB : (k + 1) * SUB, LANES:] = re * ti + im * tr
    step = 128
    for m in range(0, 64 * SUB, step):
        z = matmul3(spec[m : m + step, :], fh[...], fl[...])
        g = gain_ref[m : m + step, :]
        z = z * jnp.concatenate([g, g], axis=1)
        spec[m : m + step, :] = matmul3(z, gh[...], gl[...])
    for c in range(8):
        y = []
        for d in range(8):
            k = c + 8 * d
            tr, ti = tw_ref[0, k], tw_ref[1, k]
            re, im = spec[k * SUB : (k + 1) * SUB, :LANES], spec[k * SUB : (k + 1) * SUB, LANES:]
            y.append((re * tr + im * ti, im * tr - re * ti))
        v = dft8(y, 1)
        for b in range(8):
            mid[0, 8 * b + c], mid[1, 8 * b + c] = const_turn(v[b], b * c, 1)
    for b in range(8):
        s = dft8([(mid[0, 8 * b + c], mid[1, 8 * b + c]) for c in range(8)], 1)
        for a in range(8):
            put(0, 8 * a + b, s[a][0])
            put(1, 8 * a + b, s[a][1])


def filter_kernel(taps_ref, x_hbm, up_ref, dn_ref, w_ref, out_ref, flat, sems, xs):
    first = pl.multiple_of(pl.program_id(0) * 16 * SUB, 16 * SUB)
    gather_rows(x_hbm, first, up_ref, dn_ref, flat, sems, xs)
    taps = [taps_ref[i] for i in range(25)]

    @pl.loop(0, 16)
    def _(r):
        def store(t, value):
            out_ref[r, :, t * LANES : (t + 1) * LANES] = value

        filter_row(taps, w_ref, xs, r, store)


def phase_filter(x, up, dn, taps, weight):
    return pl.pallas_call(
        filter_kernel,
        out_shape=jax.ShapeDtypeStruct((16, 16, W), f32),
        grid=(2,),
        in_specs=[
            pl.BlockSpec(memory_space=pltpu.SMEM),
            pl.BlockSpec(memory_space=pl.ANY),
            pl.BlockSpec((2, SUB, W), lambda o: (0, o, 0)),
            pl.BlockSpec((2, SUB, W), lambda o: (0, o, 0)),
            pl.BlockSpec((WT, SUB, LANES), lambda o: (0, 0, 0)),
        ],
        out_specs=pl.BlockSpec((16, SUB, W), lambda o: (0, o, 0)),
        scratch_shapes=[
            pltpu.VMEM((WT, 16 * SUB, LANES), f32),
            pltpu.SemaphoreType.DMA((WT,)),
            pltpu.VMEM((20, WT, SUB, LANES), f32),
        ],
        compiler_params=pltpu.CompilerParams(vmem_limit_bytes=VMEM_LIMIT),
        name="phase_filter",
    )(taps, x, up, dn, weight)


def ramp_kernel(sizes, own_ref, opp_ref, tw_ref, gain_ref, fh, fl, gh, gl, out_ref, compact, sig, mid, spec):
    shift, off = W - sizes[0], sizes[1]
    for side in range(2):
        rows = slice(side * SUB, (side + 1) * SUB)

        def put(t, v):
            compact[side, t] = v

        def add(t, v):
            compact[side, t] = compact[side, t] + v

        stitch(
            lambda t: own_ref[0, rows, t * LANES : (t + 1) * LANES],
            lambda t: opp_ref[0, rows, t * LANES : (t + 1) * LANES],
            put,
            add,
            shift,
        )
        place(lambda t: compact[side, t], sig, side, off)

    def write(side, n, value):
        out_ref[0, side * SUB : (side + 1) * SUB, n * LANES : (n + 1) * LANES] = value

    ramp(sig, mid, spec, tw_ref, gain_ref, fh, fl, gh, gl, write)


def ramp_scratch():
    return [
        pltpu.VMEM((2, ST + 2, SUB, LANES), f32),
        pltpu.VMEM((2, 64, SUB, LANES), f32),
        pltpu.VMEM((64 * SUB, 2 * LANES), f32),
    ]


def constants():
    twiddle, gain, forward = tables()
    fh, fl = split(forward)
    gh, gl = split(forward.T.copy())
    return [jnp.asarray(v) for v in (twiddle, gain, fh, fl, gh, gl)]


def whole(shape):
    return pl.BlockSpec(shape, lambda *_: (0,) * len(shape))


def stitch_and_ramp(parts, sizes):
    consts = constants()
    return pl.pallas_call(
        ramp_kernel,
        out_shape=jax.ShapeDtypeStruct((1, 128, S), f32),
        grid=(8,),
        in_specs=[
            pl.BlockSpec(memory_space=pltpu.SMEM),
            pl.BlockSpec((1, 16, W), lambda d: (d, 0, 0)),
            pl.BlockSpec((1, 16, W), lambda d: (d + 8, 0, 0)),
        ]
        + [whole(v.shape) for v in consts],
        out_specs=pl.BlockSpec((1, 16, S), lambda d: (0, d, 0)),
        scratch_shapes=[pltpu.VMEM((2, CT, SUB, LANES), f32)] + ramp_scratch(),
        compiler_params=pltpu.CompilerParams(vmem_limit_bytes=VMEM_LIMIT),
        name="stitch_and_ramp",
    )(sizes, parts, parts, *consts)


def shards(projections, phase_kernel, correlation, offset):
    size = lax.axis_size("row")
    up = [(i, i + 1) for i in range(size - 1)]
    down = [(i + 1, i) for i in range(size - 1)]
    before = lax.ppermute(jnp.swapaxes(projections[:, 14:16, :], 0, 1), "row", up)
    after = lax.ppermute(jnp.swapaxes(projections[:, 0:2, :], 0, 1), "row", down)
    column = (jnp.arange(W, dtype=f32) + 0.5) / correlation[0].astype(f32)
    weight = jnp.minimum(column, 1.0).reshape(WT, 1, LANES)
    weight = jnp.broadcast_to(weight, (WT, SUB, LANES))
    sizes = jnp.concatenate([correlation, offset])
    filtered = phase_filter(projections.reshape(256, W), before, after, phase_kernel.reshape(25), weight)
    parts = lax.all_to_all(filtered, "ang", split_axis=0, concat_axis=0, tiled=True)
    return stitch_and_ramp(parts, sizes)


def solution(mesh):
    return jax.shard_map(
        shards,
        mesh=mesh,
        in_specs=(P("ang", "row", None), P(), P(), P()),
        out_specs=P(("row", "ang"), None, None),
        check_vma=False,
    )
```

```python
import functools
import math

import jax
import jax.numpy as jnp
import numpy as np
from jax import lax
from jax.experimental import pallas as pl
from jax.experimental.pallas import tpu as pltpu
from jax.sharding import PartitionSpec as P

W = 4608
S = 8192
LANES = 128
SUB = 8
WT = W // LANES
ST = S // LANES
CT = 61
VMEM_LIMIT = 60 * 1024 * 1024

f32 = jnp.float32
bf16 = jnp.bfloat16


def tables():
    k1 = np.arange(64)
    n2 = np.arange(128)
    turn = 2 * np.pi * (k1[:, None] * n2[None, :]) / S
    twiddle = np.stack([np.cos(turn), -np.sin(turn)])
    twiddle = np.repeat(twiddle[:, :, None, :], SUB, axis=2).astype(np.float32)
    freq = k1[:, None] + 64 * n2[None, :]
    gain = 2.0 * np.minimum(freq, S - freq) / S / S
    gain = np.repeat(gain[:, None, :], SUB, axis=1).reshape(64 * SUB, 128).astype(np.float32)
    angle = 2 * np.pi * ((n2[:, None] * n2[None, :]) % 128) / 128
    c, s = np.cos(angle), np.sin(angle)
    forward = np.block([[c, -s], [s, c]]).astype(np.float32)
    return twiddle, gain, forward


def split(matrix):
    high = matrix.astype(jnp.bfloat16)
    low = (matrix - high.astype(np.float32)).astype(jnp.bfloat16)
    return high, low


def cadd(a, b):
    return (a[0] + b[0], a[1] + b[1])


def csub(a, b):
    return (a[0] - b[0], a[1] - b[1])


def turn_quarter(a, sign):
    return (-a[1], a[0]) if sign > 0 else (a[1], -a[0])


def dft4(x0, x1, x2, x3, sign):
    a0, a1 = cadd(x0, x2), csub(x0, x2)
    a2, a3 = cadd(x1, x3), turn_quarter(csub(x1, x3), sign)
    return cadd(a0, a2), cadd(a1, a3), csub(a0, a2), csub(a1, a3)


def dft8(x, sign):
    e = dft4(x[0], x[2], x[4], x[6], sign)
    o = dft4(x[1], x[3], x[5], x[7], sign)
    h = math.sqrt(0.5)
    r, m = o[1]
    o1 = ((r - m) * h, (m + r) * h) if sign > 0 else ((r + m) * h, (m - r) * h)
    o2 = turn_quarter(o[2], sign)
    r, m = o[3]
    o3 = ((r + m) * -h, (r - m) * h) if sign > 0 else ((m - r) * h, (r + m) * -h)
    odd = (o[0], o1, o2, o3)
    return [cadd(e[k], odd[k]) for k in range(4)] + [csub(e[k], odd[k]) for k in range(4)]


def const_turn(a, count, sign):
    count %= 64
    if count == 0:
        return a
    c = math.cos(2 * math.pi * count / 64)
    s = sign * math.sin(2 * math.pi * count / 64)
    return (a[0] * c - a[1] * s, a[0] * s + a[1] * c)


def lane_index():
    return lax.broadcasted_iota(jnp.int32, (SUB, LANES), 1)


def gather_rows(x_hbm, first, halo_ref, flat, sems, xs):
    copies = [
        pltpu.make_async_copy(
            x_hbm.at[first : first + 16 * SUB, t * LANES : (t + 1) * LANES], flat.at[t], sems.at[t]
        )
        for t in range(WT)
    ]
    for copy in copies:
        copy.start()
    for r in range(2):
        for t in range(WT):
            cols = slice(t * LANES, (t + 1) * LANES)
            xs[r, t] = halo_ref[0, r, :, cols]
            xs[18 + r, t] = halo_ref[0, r, :, cols]

    for copy in copies:
        copy.wait()

    @pl.loop(0, 16)
    def _(r):
        for t in range(WT):
            xs[r + 2, t] = flat[t, pl.ds(r, SUB, stride=16), :]


def filter_row(taps, w_ref, xs, r, store):
    lane = lane_index()
    zero = jnp.zeros((SUB, LANES), f32)
    r0, r1, left, right3, right4 = zero, zero, None, None, None
    for t in range(WT + 1):
        if t < WT:
            rows = [xs[r + i, t] for i in range(5)]
            acc = []
            for j in range(5):
                total = taps[j] * rows[0]
                for i in range(1, 5):
                    total = total + taps[5 * i + j] * rows[i]
                acc.append(total)
            n0, n1 = pltpu.roll(acc[0], 2, 1), pltpu.roll(acc[1], 1, 1)
            n3, n4 = pltpu.roll(acc[3], LANES - 1, 1), pltpu.roll(acc[4], LANES - 2, 1)
        else:
            n3 = n4 = zero
        if t > 0:
            value = left + jnp.where(lane < LANES - 1, right3, n3) + jnp.where(lane < LANES - 2, right4, n4)
            store(t - 1, value * w_ref[t - 1])
        if t < WT:
            left = acc[2] + jnp.where(lane >= 2, n0, r0) + jnp.where(lane >= 1, n1, r1)
            r0, r1, right3, right4 = n0, n1, n3, n4


def stitch(own, opp, put, add, shift):
    lane = lane_index()
    backwards = LANES - 1 - lane
    zero = jnp.zeros((SUB, LANES), f32)
    for t in range(CT):
        put(t, jnp.take_along_axis(opp(WT - 1 - t), backwards, axis=1) if t < WT else zero)
    whole, part = shift // LANES, lax.rem(shift, LANES)
    before = zero
    for t in range(WT + 1):
        now = pltpu.roll(own(t), part, 1) if t < WT else zero
        add(whole + t, jnp.where(lane >= part, now, before))
        before = now


def place(source, sig, side, shift):
    lane = lane_index()
    zero = jnp.zeros((SUB, LANES), f32)
    whole, part = shift // LANES, lax.rem(shift, LANES)
    for t in range(4):
        sig[side, t] = zero
        sig[side, ST - 4 + t] = zero
    before = zero
    for t in range(CT + 1):
        now = pltpu.roll(source(t), part, 1) if t < CT else zero
        sig[side, whole + t] = jnp.where(lane >= part, now, before)
        before = now


def matmul3(x, high, low):
    xh = x.astype(bf16)
    xl = (x - xh.astype(f32)).astype(bf16)
    dot = functools.partial(jnp.dot, preferred_element_type=f32)
    return dot(xh, low) + dot(xl, high) + dot(xh, high)


def ramp(sig, mid, spec, tw_ref, gain_ref, fh, fl, gh, gl, put):
    for b in range(8):
        x = dft8([(sig[0, 8 * a + b], sig[1, 8 * a + b]) for a in range(8)], -1)
        for c in range(8):
            mid[0, 8 * b + c], mid[1, 8 * b + c] = const_turn(x[c], b * c, -1)
    for c in range(8):
        y = dft8([(mid[0, 8 * b + c], mid[1, 8 * b + c]) for b in range(8)], -1)
        for d in range(8):
            k = c + 8 * d
            tr, ti = tw_ref[0, k], tw_ref[1, k]
            re, im = y[d]
            spec[k * SUB : (k + 1) * SUB, :LANES] = re * tr - im * ti
            spec[k * SUB : (k + 1) * SUB, LANES:] = re * ti + im * tr
    step = 128
    for m in range(0, 64 * SUB, step):
        z = matmul3(spec[m : m + step, :], fh[...], fl[...])
        g = gain_ref[m : m + step, :]
        z = z * jnp.concatenate([g, g], axis=1)
        spec[m : m + step, :] = matmul3(z, gh[...], gl[...])
    for c in range(8):
        y = []
        for d in range(8):
            k = c + 8 * d
            tr, ti = tw_ref[0, k], tw_ref[1, k]
            re, im = spec[k * SUB : (k + 1) * SUB, :LANES], spec[k * SUB : (k + 1) * SUB, LANES:]
            y.append((re * tr + im * ti, im * tr - re * ti))
        v = dft8(y, 1)
        for b in range(8):
            mid[0, 8 * b + c], mid[1, 8 * b + c] = const_turn(v[b], b * c, 1)
    for b in range(8):
        s = dft8([(mid[0, 8 * b + c], mid[1, 8 * b + c]) for c in range(8)], 1)
        for a in range(8):
            put(0, 8 * a + b, s[a][0])
            put(1, 8 * a + b, s[a][1])


def whole(shape):
    return pl.BlockSpec(shape, lambda *_: (0,) * len(shape))


def cost(us):
    return pl.CostEstimate(flops=int(us * 1.15e7), bytes_accessed=1 << 12, transcendentals=0)


def halo_kernel(info, x_ref, out_ref):
    last = info[0] > 0
    for r in range(2):
        for t in range(WT):
            cols = slice(t * LANES, (t + 1) * LANES)
            out_ref[0, r, :, cols] = jnp.where(last, x_ref[:, 6 + r, cols], x_ref[:, r, cols])


def edge_rows(x, last, octet, count):
    return pl.pallas_call(
        halo_kernel,
        out_shape=jax.ShapeDtypeStruct((count, 2, SUB, W), f32),
        grid_spec=pltpu.PrefetchScalarGridSpec(
            num_scalar_prefetch=1,
            grid=(count,),
            in_specs=[pl.BlockSpec((SUB, SUB, W), lambda o, last: (octet + o, last[0], 0))],
            out_specs=pl.BlockSpec((1, 2, SUB, W), lambda o, last: (o, 0, 0, 0)),
        ),
        compiler_params=pltpu.CompilerParams(vmem_limit_bytes=VMEM_LIMIT),
        cost_estimate=cost(1.0 * count),
        name="edge_rows",
    )(last, x)


def nothing(*refs):
    pass


def gate(values, deps):
    anywhere = pl.BlockSpec(memory_space=pl.ANY)
    return pl.pallas_call(
        nothing,
        out_shape=[jax.ShapeDtypeStruct(v.shape, v.dtype) for v in values],
        in_specs=[anywhere] * (len(values) + len(deps)),
        out_specs=[anywhere] * len(values),
        input_output_aliases={i: i for i in range(len(values))},
        cost_estimate=cost(0.3),
        name="gate",
    )(*values, *deps)


def filter_kernel(octet, info, taps_ref, x_hbm, halo_ref, w_ref, *rest):
    outs, (flat, sems, xs) = rest[-7:-3], rest[-3:]
    first = octet * 16 * SUB
    gather_rows(x_hbm, first, halo_ref, flat, sems, xs)
    taps = [taps_ref[i] for i in range(25)]
    for s in range(4):

        @pl.loop(0, 2)
        def _(c):
            def store(t, value):
                outs[s][0, c, t] = value

            r = lax.rem(info[0] + s, 4) * 4 + info[1] * 2 + c
            filter_row(taps, w_ref, xs, r, store)


def phase_filter(x, halo, taps, weight, info, octet, deps=()):
    block = (1, 2, WT, SUB, LANES)
    at = octet if halo.shape[0] > 1 else 0
    anywhere = pl.BlockSpec(memory_space=pl.ANY)
    return pl.pallas_call(
        functools.partial(filter_kernel, octet),
        out_shape=[jax.ShapeDtypeStruct(block, f32)] * 4,
        grid=(1,),
        in_specs=[
            pl.BlockSpec(memory_space=pltpu.SMEM),
            pl.BlockSpec(memory_space=pltpu.SMEM),
            anywhere,
            pl.BlockSpec((1, 2, SUB, W), lambda o: (at, 0, 0, 0)),
            whole((WT, SUB, LANES)),
        ]
        + [anywhere] * len(deps),
        out_specs=[whole(block)] * 4,
        scratch_shapes=[
            pltpu.VMEM((WT, 16 * SUB, LANES), f32),
            pltpu.SemaphoreType.DMA((WT,)),
            pltpu.VMEM((20, WT, SUB, LANES), f32),
        ],
        compiler_params=pltpu.CompilerParams(vmem_limit_bytes=VMEM_LIMIT),
        cost_estimate=cost(5.0),
        name="phase_filter",
    )(info, taps, x, halo, weight, *deps)


def stitch_kernel(info, r0, r1, r2, r3, *rest):
    mine, other = rest[-2:]
    shift, y, core = W - info[0], info[2], info[4]
    for near, far, place_of in ((r0, r2, y), (r1, r3, lax.rem(y + 3, 4))):
        near_is_own = place_of < 2
        half = lax.rem(place_of, 2)
        for out, row in ((mine, core), (other, 1 - core)):

            def put(t, v):
                out[half, 0, t] = v

            def add(t, v):
                out[half, 0, t] = out[half, 0, t] + v

            stitch(
                lambda t: jnp.where(near_is_own, near[0, row, t], far[0, row, t]),
                lambda t: jnp.where(near_is_own, far[0, row, t], near[0, row, t]),
                put,
                add,
                shift,
            )


def stitch_pairs(parts, info, deps=()):
    out = jax.ShapeDtypeStruct((2, 1, CT, SUB, LANES), f32)
    return pl.pallas_call(
        stitch_kernel,
        out_shape=[out, out],
        in_specs=[pl.BlockSpec(memory_space=pltpu.SMEM)]
        + [whole((1, 2, WT, SUB, LANES))] * 4
        + [pl.BlockSpec(memory_space=pl.ANY)] * len(deps),
        out_specs=[whole((2, 1, CT, SUB, LANES))] * 2,
        grid=(1,),
        compiler_params=pltpu.CompilerParams(vmem_limit_bytes=VMEM_LIMIT),
        cost_estimate=cost(1.5),
        name="stitch_pairs",
    )(info, *parts, *deps)


def ramp_kernel(octet, info, source, tw_ref, gain_ref, fh, fl, gh, gl, *rest):
    out_ref, (sig, mid, spec) = rest[-4], rest[-3:]
    for half in range(2):
        place(lambda t: source[half, 0, t], sig, half, info[1])

    def write(half, n, value):
        out_ref[half, 0, 0, 0, :, n * LANES : (n + 1) * LANES] = value

    ramp(sig, mid, spec, tw_ref, gain_ref, fh, fl, gh, gl, write)


def constants():
    twiddle, gain, forward = tables()
    fh, fl = split(forward)
    gh, gl = split(forward.T.copy())
    return [jnp.asarray(v) for v in (twiddle, gain, fh, fl, gh, gl)]


def ramp_filter(rows, info, consts, octet, result=None, deps=()):
    count = rows.shape[1]
    anywhere = pl.BlockSpec(memory_space=pl.ANY)
    in_specs = [pl.BlockSpec((2, 1, CT, SUB, LANES), lambda o, info: (0, o, 0, 0, 0))]
    in_specs += [whole(v.shape) for v in consts] + [anywhere] * len(deps)
    operands = [rows, *consts, *deps]
    alias = {}
    if result is not None:
        alias = {1 + len(operands): 0}
        in_specs.append(anywhere)
        operands.append(result)
    return pl.pallas_call(
        functools.partial(ramp_kernel, octet),
        out_shape=jax.ShapeDtypeStruct((2, 2, 2, 2, SUB, S), f32),
        grid_spec=pltpu.PrefetchScalarGridSpec(
            num_scalar_prefetch=1,
            grid=(count,),
            in_specs=in_specs,
            out_specs=pl.BlockSpec(
                (2, 1, 1, 1, SUB, S), lambda o, info: (0, info[5], info[6], octet + o, 0, 0)
            ),
            scratch_shapes=[
                pltpu.VMEM((2, ST + 2, SUB, LANES), f32),
                pltpu.VMEM((2, 64, SUB, LANES), f32),
                pltpu.VMEM((64 * SUB, 2 * LANES), f32),
            ],
        ),
        input_output_aliases=alias,
        compiler_params=pltpu.CompilerParams(vmem_limit_bytes=VMEM_LIMIT),
        cost_estimate=cost(1.7 * count),
        name="ramp_filter",
    )(info, *operands)


def y_step(block, s):
    route = [(i, (i // 4 + s) % 4 * 4 + i % 4) for i in range(16)]
    return lax.ppermute(block, "ang", route)


def flip(block, bits):
    return lax.ppermute(block, "ang", [(i, i ^ bits) for i in range(16)])


def row_step(block, up_side):
    rows, angs = lax.axis_size("row"), lax.axis_size("ang")
    route = []
    for r in range(rows):
        for a in range(angs):
            to = r + 1 if a // 2 % 2 == up_side else r - 1
            if 0 <= to < rows:
                route.append((a * rows + r, a * rows + to))
    return lax.ppermute(block, ("ang", "row"), route)


def shards(projections, phase_kernel, correlation, offset):
    column = (jnp.arange(W, dtype=f32) + 0.5) / correlation[0].astype(f32)
    weight = jnp.minimum(column, 1.0).reshape(WT, 1, LANES)
    weight = jnp.broadcast_to(weight, (WT, SUB, LANES))
    me = lax.axis_index("ang").astype(jnp.uint32)
    y, x, core = [v.astype(jnp.int32) for v in (me >> 2, (me >> 1) & 1, me & 1)]
    to_other = jnp.stack([y, 1 - x])
    to_own = jnp.stack([y, x])

    def info(x_of, core_of):
        return jnp.stack([correlation[0], offset[0], y, x, core, x_of, core_of])

    flat = projections.reshape(256, W)
    taps = phase_kernel.reshape(25)
    consts = constants()

    def y_exchange(parts):
        return [parts[0]] + [y_step(parts[s], s) for s in (1, 2, 3)]

    near = [row_step(edge_rows(projections, x.reshape(1), o, 1), 1) for o in range(2)]
    far = row_step(edge_rows(projections, (1 - x).reshape(1), 0, 2), 0)

    same, cross = info(1 - x, core), info(1 - x, 1 - core)
    keep, swap = info(x, core), info(x, 1 - core)

    def send(rows):
        return flip(rows[0], 2), flip(rows[1], 3)

    sent_0 = phase_filter(flat, near[0], taps, weight, to_other, 0)
    parts_0 = y_exchange(sent_0)
    sent_1 = phase_filter(flat, near[1], taps, weight, to_other, 1, sent_0[1:2])
    sent_1 = [sent_1[0], *gate(sent_1[1:], parts_0[1:])]
    parts_1 = y_exchange(sent_1)
    rows_0 = stitch_pairs(parts_0, same, sent_1[1:2])
    arrived_0 = send(rows_0)
    sent_2 = phase_filter(flat, far, taps, weight, to_own, 0, [rows_0[0], sent_1[1]])
    sent_3 = phase_filter(flat, far, taps, weight, to_own, 1, [sent_2[0]])
    sent_2 = [sent_2[0], *gate(sent_2[1:], [*parts_1[1:], sent_3[0]])]
    parts_2 = y_exchange(sent_2)
    rows_1 = stitch_pairs(parts_1, same, sent_2[1:2])
    arrived_1 = send(rows_1)
    result = ramp_filter(arrived_0[0], same, consts, 0, None, [rows_1[0]])
    result = ramp_filter(arrived_0[1], cross, consts, 0, result)
    sent_3 = [sent_3[0], *gate(sent_3[1:], [*parts_2[1:], result])]
    parts_3 = y_exchange(sent_3)
    rows_2 = stitch_pairs(parts_2, keep, [sent_3[1], arrived_1[0]])
    swapped_2 = flip(rows_2[1], 1)
    result = ramp_filter(arrived_1[0], same, consts, 1, result)
    result = ramp_filter(rows_2[0], keep, consts, 0, result)
    result = ramp_filter(swapped_2, swap, consts, 0, result)
    rows_3 = stitch_pairs(parts_3, keep, [result, arrived_1[1]])
    swapped_3 = flip(rows_3[1], 1)
    result = ramp_filter(arrived_1[1], cross, consts, 1, result)
    result = ramp_filter(rows_3[0], keep, consts, 1, result)
    result = ramp_filter(swapped_3, swap, consts, 1, result)
    return result.reshape(1, 128, S)


def solution(mesh):
    return jax.shard_map(
        shards,
        mesh=mesh,
        in_specs=(P("ang", "row", None), P(), P(), P()),
        out_specs=P(("row", "ang"), None, None),
        check_vma=False,
    )
```

```python
import functools
import math

import jax
import jax.numpy as jnp
import numpy as np
from jax import lax
from jax.experimental import pallas as pl
from jax.experimental.pallas import tpu as pltpu
from jax.sharding import PartitionSpec as P

W = 4608
S = 8192
LANES = 128
SUB = 8
WT = W // LANES
ST = S // LANES
CT = 61

f32 = jnp.float32
bf16 = jnp.bfloat16


def tables():
    k1 = np.arange(64)
    n2 = np.arange(128)
    turn = 2 * np.pi * (k1[:, None] * n2[None, :]) / S
    twiddle = np.stack([np.cos(turn), -np.sin(turn)])
    twiddle = np.repeat(twiddle[:, :, None, :], SUB, axis=2).astype(np.float32)
    freq = k1[:, None] + 64 * n2[None, :]
    gain = 2.0 * np.minimum(freq, S - freq) / S / S
    gain = np.repeat(gain[:, None, :], SUB, axis=1).reshape(64 * SUB, 128).astype(np.float32)
    angle = 2 * np.pi * ((n2[:, None] * n2[None, :]) % 128) / 128
    c, s = np.cos(angle), np.sin(angle)
    forward = np.block([[c, -s], [s, c]]).astype(np.float32)
    return twiddle, gain, forward


def split(matrix):
    high = matrix.astype(jnp.bfloat16)
    low = (matrix - high.astype(np.float32)).astype(jnp.bfloat16)
    return high, low


def cadd(a, b):
    return (a[0] + b[0], a[1] + b[1])


def csub(a, b):
    return (a[0] - b[0], a[1] - b[1])


def turn_quarter(a, sign):
    return (-a[1], a[0]) if sign > 0 else (a[1], -a[0])


def dft4(x0, x1, x2, x3, sign):
    a0, a1 = cadd(x0, x2), csub(x0, x2)
    a2, a3 = cadd(x1, x3), turn_quarter(csub(x1, x3), sign)
    return cadd(a0, a2), cadd(a1, a3), csub(a0, a2), csub(a1, a3)


def dft8(x, sign):
    e = dft4(x[0], x[2], x[4], x[6], sign)
    o = dft4(x[1], x[3], x[5], x[7], sign)
    h = math.sqrt(0.5)
    r, m = o[1]
    o1 = ((r - m) * h, (m + r) * h) if sign > 0 else ((r + m) * h, (m - r) * h)
    o2 = turn_quarter(o[2], sign)
    r, m = o[3]
    o3 = ((r + m) * -h, (r - m) * h) if sign > 0 else ((m - r) * h, (r + m) * -h)
    odd = (o[0], o1, o2, o3)
    return [cadd(e[k], odd[k]) for k in range(4)] + [csub(e[k], odd[k]) for k in range(4)]


def const_turn(a, count, sign):
    count %= 64
    if count == 0:
        return a
    c = math.cos(2 * math.pi * count / 64)
    s = sign * math.sin(2 * math.pi * count / 64)
    return (a[0] * c - a[1] * s, a[0] * s + a[1] * c)


def lane_index():
    return lax.broadcasted_iota(jnp.int32, (SUB, LANES), 1)


def filter_row(taps, w_ref, xs, r, store):
    lane = lane_index()
    zero = jnp.zeros((SUB, LANES), f32)
    r0, r1, left, right3, right4 = zero, zero, None, None, None
    for t in range(WT + 1):
        if t < WT:
            rows = [xs[r + i, t] for i in range(5)]
            acc = []
            for j in range(5):
                total = taps[j] * rows[0]
                for i in range(1, 5):
                    total = total + taps[5 * i + j] * rows[i]
                acc.append(total)
            n0, n1 = pltpu.roll(acc[0], 2, 1), pltpu.roll(acc[1], 1, 1)
            n3, n4 = pltpu.roll(acc[3], LANES - 1, 1), pltpu.roll(acc[4], LANES - 2, 1)
        else:
            n3 = n4 = zero
        if t > 0:
            value = left + jnp.where(lane < LANES - 1, right3, n3) + jnp.where(lane < LANES - 2, right4, n4)
            store(t - 1, value * w_ref[t - 1])
        if t < WT:
            left = acc[2] + jnp.where(lane >= 2, n0, r0) + jnp.where(lane >= 1, n1, r1)
            r0, r1, right3, right4 = n0, n1, n3, n4


def stitch(own, opp, put, add, shift):
    lane = lane_index()
    backwards = LANES - 1 - lane
    zero = jnp.zeros((SUB, LANES), f32)
    for t in range(CT):
        put(t, jnp.take_along_axis(opp(WT - 1 - t), backwards, axis=1) if t < WT else zero)
    whole, part = shift // LANES, lax.rem(shift, LANES)
    before = zero
    for t in range(WT + 1):
        now = pltpu.roll(own(t), part, 1) if t < WT else zero
        add(whole + t, jnp.where(lane >= part, now, before))
        before = now


def place(source, sig, side, shift):
    lane = lane_index()
    zero = jnp.zeros((SUB, LANES), f32)
    whole, part = shift // LANES, lax.rem(shift, LANES)
    for t in range(4):
        sig[side, t] = zero
        sig[side, ST - 4 + t] = zero
    before = zero
    for t in range(CT + 1):
        now = pltpu.roll(source(t), part, 1) if t < CT else zero
        sig[side, whole + t] = jnp.where(lane >= part, now, before)
        before = now


def matmul3(x, high, low):
    xh = x.astype(bf16)
    xl = (x - xh.astype(f32)).astype(bf16)
    dot = functools.partial(jnp.dot, preferred_element_type=f32)
    return dot(xh, low) + dot(xl, high) + dot(xh, high)


def ramp(sig, mid, spec, tw_ref, gain_ref, fh, fl, gh, gl, put):
    for b in range(8):
        x = dft8([(sig[0, 8 * a + b], sig[1, 8 * a + b]) for a in range(8)], -1)
        for c in range(8):
            mid[0, 8 * b + c], mid[1, 8 * b + c] = const_turn(x[c], b * c, -1)
    for c in range(8):
        y = dft8([(mid[0, 8 * b + c], mid[1, 8 * b + c]) for b in range(8)], -1)
        for d in range(8):
            k = c + 8 * d
            tr, ti = tw_ref[0, k], tw_ref[1, k]
            re, im = y[d]
            spec[k * SUB : (k + 1) * SUB, :LANES] = re * tr - im * ti
            spec[k * SUB : (k + 1) * SUB, LANES:] = re * ti + im * tr
    step = 128
    for m in range(0, 64 * SUB, step):
        z = matmul3(spec[m : m + step, :], fh[...], fl[...])
        g = gain_ref[m : m + step, :]
        z = z * jnp.concatenate([g, g], axis=1)
        spec[m : m + step, :] = matmul3(z, gh[...], gl[...])
    for c in range(8):
        y = []
        for d in range(8):
            k = c + 8 * d
            tr, ti = tw_ref[0, k], tw_ref[1, k]
            re, im = spec[k * SUB : (k + 1) * SUB, :LANES], spec[k * SUB : (k + 1) * SUB, LANES:]
            y.append((re * tr + im * ti, im * tr - re * ti))
        v = dft8(y, 1)
        for b in range(8):
            mid[0, 8 * b + c], mid[1, 8 * b + c] = const_turn(v[b], b * c, 1)
    for b in range(8):
        s = dft8([(mid[0, 8 * b + c], mid[1, 8 * b + c]) for c in range(8)], 1)
        for a in range(8):
            put(0, 8 * a + b, s[a][0])
            put(1, 8 * a + b, s[a][1])


def whole(shape):
    return pl.BlockSpec(shape, lambda *_: (0,) * len(shape))


def cost(us):
    return pl.CostEstimate(flops=int(us * 1.15e7), bytes_accessed=1 << 12, transcendentals=0)


def limit(mib):
    return pltpu.CompilerParams(vmem_limit_bytes=mib * 1024 * 1024)


SMEM = pl.BlockSpec(memory_space=pltpu.SMEM)
ANYWHERE = pl.BlockSpec(memory_space=pl.ANY)
TOKEN = jax.ShapeDtypeStruct((SUB, LANES), f32)
TOKEN_SPEC = whole((SUB, LANES))
ROWS = (16, WT, SUB, LANES)


def gather_kernel(x_hbm, out_ref, token, flat, sems):
    octet = pl.program_id(0)
    first = pl.multiple_of(octet * 16 * SUB, 16 * SUB)
    copies = [
        pltpu.make_async_copy(
            x_hbm.at[pl.ds(first, 16 * SUB), t * LANES : (t + 1) * LANES], flat.at[t], sems.at[t]
        )
        for t in range(WT)
    ]
    for copy in copies:
        copy.start()
    for copy in copies:
        copy.wait()
    for r in range(16):
        for t in range(WT):
            out_ref[0, r, t] = flat[t, pl.ds(r, SUB, stride=16), :]
    token[...] = jnp.zeros_like(token)


def gather_rows(x):
    return pl.pallas_call(
        gather_kernel,
        out_shape=[jax.ShapeDtypeStruct((2,) + ROWS, f32), TOKEN],
        grid=(2,),
        in_specs=[ANYWHERE],
        out_specs=[pl.BlockSpec((1,) + ROWS, lambda o: (o, 0, 0, 0, 0)), TOKEN_SPEC],
        scratch_shapes=[pltpu.VMEM((WT, 16 * SUB, LANES), f32), pltpu.SemaphoreType.DMA((WT,))],
        compiler_params=limit(16),
        cost_estimate=cost(3.0),
        name="gather_rows",
    )(x)


def filter_kernel(octet, other, info, taps_ref, xt_hbm, halo_ref, *rest):
    outs, token, edge = rest[-11:-7], rest[-7], rest[-6]
    in_sem, xs, ys, weight, out_sems = rest[-5:]
    step = pl.program_id(0)
    load = pltpu.make_async_copy(xt_hbm.at[octet + step], xs.at[2:18], in_sem)
    load.start()
    for r in range(2):
        for t in range(WT):
            if other:
                value = halo_ref[r, :, t * LANES : (t + 1) * LANES]
            else:
                value = halo_ref[0, r, t]
            xs[r, t] = value
            xs[18 + r, t] = value
    taps = [taps_ref[i, j] for i in range(5) for j in range(5)]
    overlap = info[0].astype(f32)
    lane = lane_index().astype(f32) + 0.5
    for t in range(WT):
        weight[t] = jnp.minimum((lane + t * LANES) / overlap, 1.0)
    token[...] = jnp.zeros_like(token)
    x_of = 1 - info[3] if other else info[3]
    load.wait()
    if other:
        top = 2 + 14 * (1 - info[3])
        for r in range(2):
            for t in range(WT):
                edge[0, r, t] = xs[top + r, t]
    else:
        edge[...] = jnp.zeros_like(edge)

    @pl.loop(0, 8)
    def _(i):
        def store(t, value):
            ys[i, t] = value

        r = lax.rem(info[2] + i // 2, 4) * 4 + x_of * 2 + lax.rem(i, 2)
        filter_row(taps, weight, xs, r, store)
        for s in range(4):

            @pl.when(i == 2 * s + 1)
            def _():
                pltpu.make_async_copy(ys.at[2 * s : 2 * s + 2], outs[s].at[step], out_sems.at[s]).start()

    for s in range(4):
        pltpu.make_async_copy(ys.at[2 * s : 2 * s + 2], outs[s].at[step], out_sems.at[s]).wait()


def phase_filter(xt, halo, taps, info, octet, count, other, deps=()):
    if other:
        halo_spec = pl.BlockSpec((2, SUB, W), lambda o: (0, octet + o, 0))
        edge = (1, 2, WT, SUB, LANES)
    else:
        halo_spec = pl.BlockSpec((1, 2, WT, SUB, LANES), lambda o: (octet + o, 0, 0, 0, 0))
        edge = (SUB, LANES)
    return pl.pallas_call(
        functools.partial(filter_kernel, octet, other),
        out_shape=[jax.ShapeDtypeStruct((count, 2, WT, SUB, LANES), f32)] * 4
        + [TOKEN, jax.ShapeDtypeStruct(edge, f32)],
        grid=(count,),
        in_specs=[SMEM, SMEM, ANYWHERE, halo_spec] + [ANYWHERE] * len(deps),
        out_specs=[ANYWHERE] * 4 + [TOKEN_SPEC, whole(edge)],
        scratch_shapes=[
            pltpu.SemaphoreType.DMA,
            pltpu.VMEM((20, WT, SUB, LANES), f32),
            pltpu.VMEM((8, WT, SUB, LANES), f32),
            pltpu.VMEM((WT, SUB, LANES), f32),
            pltpu.SemaphoreType.DMA((4,)),
        ],
        compiler_params=limit(12),
        cost_estimate=cost(5.0),
        name="phase_filter",
    )(info, taps, xt, halo, *deps)


def stitch_kernel(info, r0, r1, r2, r3, *rest):
    mine, crossing, token = rest[-3:]
    token[...] = jnp.zeros_like(token)
    shift, y, core = W - info[0], info[2], info[4]
    for near, far, place_of in ((r0, r2, y), (r1, r3, lax.rem(y + 3, 4))):
        near_is_own = place_of < 2
        half = lax.rem(place_of, 2)
        for out, row in ((mine, core), (crossing, 1 - core)):

            def put(t, v):
                out[half, 0, t] = v

            def add(t, v):
                out[half, 0, t] = out[half, 0, t] + v

            stitch(
                lambda t: jnp.where(near_is_own, near[0, row, t], far[0, row, t]),
                lambda t: jnp.where(near_is_own, far[0, row, t], near[0, row, t]),
                put,
                add,
                shift,
            )


def stitch_pairs(parts, info, deps=()):
    count = parts[0].shape[0]
    out = jax.ShapeDtypeStruct((2, count, CT, SUB, LANES), f32)
    return pl.pallas_call(
        stitch_kernel,
        out_shape=[out, out, TOKEN],
        in_specs=[SMEM]
        + [pl.BlockSpec((1, 2, WT, SUB, LANES), lambda o: (o, 0, 0, 0, 0))] * 4
        + [ANYWHERE] * len(deps),
        out_specs=[pl.BlockSpec((2, 1, CT, SUB, LANES), lambda o: (0, o, 0, 0, 0))] * 2 + [TOKEN_SPEC],
        grid=(count,),
        compiler_params=limit(8),
        cost_estimate=cost(1.5),
        name="stitch_pairs",
    )(info, *parts, *deps)


SLOTS = 5


def ramp_kernel(sources, info, *refs):
    rows, (tw_ref, gain_ref, fh, fl, gh, gl) = refs[:sources], refs[sources : sources + 6]
    out_ref, token, (sig, mid, spec) = refs[-5], refs[-4], refs[-3:]
    token[...] = jnp.zeros_like(token)
    steps = [(source, which) for source in rows for which in range(source.shape[1])]
    for n, (source, which) in enumerate(steps):

        @pl.when(pl.program_id(0) == n)
        def _():
            for half in range(2):
                place(lambda t: source[half, which, t], sig, half, info[1])

    def write(half, n, value):
        out_ref[half, 0, 0, 0, :, n * LANES : (n + 1) * LANES] = value

    ramp(sig, mid, spec, tw_ref, gain_ref, fh, fl, gh, gl, write)


def constants():
    twiddle, gain, forward = tables()
    fh, fl = split(forward)
    gh, gl = split(forward.T.copy())
    return [jnp.asarray(v) for v in (twiddle, gain, fh, fl, gh, gl)]


def ramp_filter(rows, info, consts, slot, result=None, deps=()):
    steps = sum(v.shape[1] for v in rows)
    local = pl.BlockSpec(memory_space=pltpu.VMEM)
    in_specs = [local] * (len(rows) + len(consts)) + [ANYWHERE] * len(deps)
    operands = [*rows, *consts, *deps]
    alias = {}
    if result is not None:
        alias = {1 + len(operands): 0}
        in_specs.append(ANYWHERE)
        operands.append(result)

    def target(i, info):
        at = SLOTS + 3 * (slot + i)
        return (0, info[at], info[at + 1], info[at + 2], 0, 0)

    return pl.pallas_call(
        functools.partial(ramp_kernel, len(rows)),
        out_shape=[jax.ShapeDtypeStruct((2, 2, 2, 2, SUB, S), f32), TOKEN],
        grid_spec=pltpu.PrefetchScalarGridSpec(
            num_scalar_prefetch=1,
            grid=(steps,),
            in_specs=in_specs,
            out_specs=[pl.BlockSpec((2, 1, 1, 1, SUB, S), target), whole((SUB, LANES))],
            scratch_shapes=[
                pltpu.VMEM((2, ST + 2, SUB, LANES), f32),
                pltpu.VMEM((2, 64, SUB, LANES), f32),
                pltpu.VMEM((64 * SUB, 2 * LANES), f32),
            ],
        ),
        input_output_aliases=alias,
        compiler_params=limit(16),
        cost_estimate=cost(2.0),
        name="ramp_filter",
    )(info, *operands)


def y_step(block, s):
    route = [(i, (i // 4 + s) % 4 * 4 + i % 4) for i in range(16)]
    return lax.ppermute(block, "ang", route)


def flip(block, bits):
    return lax.ppermute(block, "ang", [(i, i ^ bits) for i in range(16)])


def row_step(block, up_side):
    rows, angs = lax.axis_size("row"), lax.axis_size("ang")
    route = []
    for r in range(rows):
        for a in range(angs):
            to = r + 1 if a // 2 % 2 == up_side else r - 1
            if 0 <= to < rows:
                route.append((a * rows + r, a * rows + to))
    return lax.ppermute(block, ("ang", "row"), route)


def shards(projections, phase_kernel, correlation, offset):
    me = lax.axis_index("ang").astype(jnp.uint32)
    y, x, core = [v.astype(jnp.int32) for v in (me >> 2, (me >> 1) & 1, me & 1)]
    slots = []
    for x_of, core_of, octet in (
        (1 - x, core, 0),
        (1 - x, 1 - core, 0),
        (x, core, 0),
        (x, core, 1),
        (1 - x, core, 1),
        (x, 1 - core, 0),
        (x, 1 - core, 1),
        (1 - x, 1 - core, 1),
    ):
        slots += [x_of, core_of, jnp.int32(octet)]
    info = jnp.stack([correlation[0], offset[0], y, x, core] + slots)
    consts = constants()

    def y_exchange(parts):
        return [parts[0]] + [y_step(parts[s], s) for s in (1, 2, 3)]

    def send(rows):
        return flip(rows[0], 2), flip(rows[1], 3)

    near = lax.dynamic_slice_in_dim(projections, 14 * x, 2, axis=1)
    near = row_step(jnp.swapaxes(near, 0, 1), 1)
    xt, gathered = gather_rows(projections.reshape(256, W))
    *sent_0, done, edge_0 = phase_filter(xt, near, phase_kernel, info, 0, 1, True)
    parts_0 = y_exchange(sent_0)
    *sent_1, done, edge_1 = phase_filter(xt, near, phase_kernel, info, 1, 1, True, [done])
    parts_1 = y_exchange(sent_1)
    far = row_step(jnp.concatenate([edge_0, edge_1], axis=0), 0)
    *rows_0, done = stitch_pairs(parts_0, info, [done])
    arrived_0 = send(rows_0)
    *sent_2, done, _ = phase_filter(xt, far, phase_kernel, info, 0, 2, False, [done])
    parts_2 = y_exchange(sent_2)
    *rows_1, done = stitch_pairs(parts_1, info, [done])
    arrived_1 = send(rows_1)
    result, done = ramp_filter(arrived_0, info, consts, 0, None, [done])
    *rows_2, done = stitch_pairs(parts_2, info, [done, arrived_1[0][0, 0, 0]])
    swapped = flip(rows_2[1], 1)
    result, done = ramp_filter([rows_2[0], arrived_1[0]], info, consts, 2, result)
    result, done = ramp_filter([swapped, arrived_1[1]], info, consts, 5, result)
    return result.reshape(1, 128, S)


def solution(mesh):
    return jax.shard_map(
        shards,
        mesh=mesh,
        in_specs=(P("ang", "row", None), P(), P(), P()),
        out_specs=P(("row", "ang"), None, None),
        check_vma=False,
    )
```

```python
import functools
import math

import jax
import jax.numpy as jnp
import numpy as np
from jax import lax
from jax.experimental import pallas as pl
from jax.experimental.pallas import tpu as pltpu
from jax.sharding import PartitionSpec as P

W = 4608
S = 8192
LANES = 128
SUB = 8
WT = W // LANES
ST = S // LANES
CT = 61

f32 = jnp.float32
bf16 = jnp.bfloat16


def tables():
    k1 = np.arange(64)
    n2 = np.arange(128)
    turn = 2 * np.pi * (k1[:, None] * n2[None, :]) / S
    twiddle = np.stack([np.cos(turn), -np.sin(turn)])
    twiddle = np.repeat(twiddle[:, :, None, :], SUB, axis=2).astype(np.float32)
    freq = k1[:, None] + 64 * n2[None, :]
    gain = 2.0 * np.minimum(freq, S - freq) / S / S
    gain = np.repeat(gain[:, None, :], SUB, axis=1).reshape(64 * SUB, 128).astype(np.float32)
    angle = 2 * np.pi * ((n2[:, None] * n2[None, :]) % 128) / 128
    c, s = np.cos(angle), np.sin(angle)
    forward = np.block([[c, -s], [s, c]]).astype(np.float32)
    return twiddle, gain, forward


def split(matrix):
    high = matrix.astype(jnp.bfloat16)
    low = (matrix - high.astype(np.float32)).astype(jnp.bfloat16)
    return high, low


def cadd(a, b):
    return (a[0] + b[0], a[1] + b[1])


def csub(a, b):
    return (a[0] - b[0], a[1] - b[1])


def turn_quarter(a, sign):
    return (-a[1], a[0]) if sign > 0 else (a[1], -a[0])


def dft4(x0, x1, x2, x3, sign):
    a0, a1 = cadd(x0, x2), csub(x0, x2)
    a2, a3 = cadd(x1, x3), turn_quarter(csub(x1, x3), sign)
    return cadd(a0, a2), cadd(a1, a3), csub(a0, a2), csub(a1, a3)


def dft8(x, sign):
    e = dft4(x[0], x[2], x[4], x[6], sign)
    o = dft4(x[1], x[3], x[5], x[7], sign)
    h = math.sqrt(0.5)
    r, m = o[1]
    o1 = ((r - m) * h, (m + r) * h) if sign > 0 else ((r + m) * h, (m - r) * h)
    o2 = turn_quarter(o[2], sign)
    r, m = o[3]
    o3 = ((r + m) * -h, (r - m) * h) if sign > 0 else ((m - r) * h, (r + m) * -h)
    odd = (o[0], o1, o2, o3)
    return [cadd(e[k], odd[k]) for k in range(4)] + [csub(e[k], odd[k]) for k in range(4)]


def const_turn(a, count, sign):
    count %= 64
    if count == 0:
        return a
    c = math.cos(2 * math.pi * count / 64)
    s = sign * math.sin(2 * math.pi * count / 64)
    return (a[0] * c - a[1] * s, a[0] * s + a[1] * c)


def lane_index():
    return lax.broadcasted_iota(jnp.int32, (SUB, LANES), 1)


def filter_row(taps, w_ref, xs, r, store):
    lane = lane_index()
    zero = jnp.zeros((SUB, LANES), f32)
    r0, r1, left, right3, right4 = zero, zero, None, None, None
    for t in range(WT + 1):
        if t < WT:
            rows = [xs[r + i, t] for i in range(5)]
            acc = []
            for j in range(5):
                total = taps[j] * rows[0]
                for i in range(1, 5):
                    total = total + taps[5 * i + j] * rows[i]
                acc.append(total)
            n0, n1 = pltpu.roll(acc[0], 2, 1), pltpu.roll(acc[1], 1, 1)
            n3, n4 = pltpu.roll(acc[3], LANES - 1, 1), pltpu.roll(acc[4], LANES - 2, 1)
        else:
            n3 = n4 = zero
        if t > 0:
            value = left + jnp.where(lane < LANES - 1, right3, n3) + jnp.where(lane < LANES - 2, right4, n4)
            store(t - 1, value * w_ref[t - 1])
        if t < WT:
            left = acc[2] + jnp.where(lane >= 2, n0, r0) + jnp.where(lane >= 1, n1, r1)
            r0, r1, right3, right4 = n0, n1, n3, n4


def stitch(own, opp, put, add, shift):
    lane = lane_index()
    backwards = LANES - 1 - lane
    zero = jnp.zeros((SUB, LANES), f32)
    for t in range(CT):
        put(t, jnp.take_along_axis(opp(WT - 1 - t), backwards, axis=1) if t < WT else zero)
    whole, part = shift // LANES, lax.rem(shift, LANES)
    before = zero
    for t in range(WT + 1):
        now = pltpu.roll(own(t), part, 1) if t < WT else zero
        add(whole + t, jnp.where(lane >= part, now, before))
        before = now


def place(source, sig, side, shift):
    lane = lane_index()
    zero = jnp.zeros((SUB, LANES), f32)
    whole, part = shift // LANES, lax.rem(shift, LANES)
    for t in range(4):
        sig[side, t] = zero
        sig[side, ST - 4 + t] = zero
    before = zero
    for t in range(CT + 1):
        now = pltpu.roll(source(t), part, 1) if t < CT else zero
        sig[side, whole + t] = jnp.where(lane >= part, now, before)
        before = now


def matmul3(x, high, low):
    xh = x.astype(bf16)
    xl = (x - xh.astype(f32)).astype(bf16)
    dot = functools.partial(jnp.dot, preferred_element_type=f32)
    return dot(xh, low) + dot(xl, high) + dot(xh, high)


def ramp(sig, mid, spec, tw_ref, gain_ref, fh, fl, gh, gl, put):
    for b in range(8):
        x = dft8([(sig[0, 8 * a + b], sig[1, 8 * a + b]) for a in range(8)], -1)
        for c in range(8):
            mid[0, 8 * b + c], mid[1, 8 * b + c] = const_turn(x[c], b * c, -1)
    for c in range(8):
        y = dft8([(mid[0, 8 * b + c], mid[1, 8 * b + c]) for b in range(8)], -1)
        for d in range(8):
            k = c + 8 * d
            tr, ti = tw_ref[0, k], tw_ref[1, k]
            re, im = y[d]
            spec[k * SUB : (k + 1) * SUB, :LANES] = re * tr - im * ti
            spec[k * SUB : (k + 1) * SUB, LANES:] = re * ti + im * tr
    step = 128
    for m in range(0, 64 * SUB, step):
        z = matmul3(spec[m : m + step, :], fh[...], fl[...])
        g = gain_ref[m : m + step, :]
        z = z * jnp.concatenate([g, g], axis=1)
        spec[m : m + step, :] = matmul3(z, gh[...], gl[...])
    for c in range(8):
        y = []
        for d in range(8):
            k = c + 8 * d
            tr, ti = tw_ref[0, k], tw_ref[1, k]
            re, im = spec[k * SUB : (k + 1) * SUB, :LANES], spec[k * SUB : (k + 1) * SUB, LANES:]
            y.append((re * tr + im * ti, im * tr - re * ti))
        v = dft8(y, 1)
        for b in range(8):
            mid[0, 8 * b + c], mid[1, 8 * b + c] = const_turn(v[b], b * c, 1)
    for b in range(8):
        s = dft8([(mid[0, 8 * b + c], mid[1, 8 * b + c]) for c in range(8)], 1)
        for a in range(8):
            put(0, 8 * a + b, s[a][0])
            put(1, 8 * a + b, s[a][1])


def whole(shape):
    return pl.BlockSpec(shape, lambda *_: (0,) * len(shape))


def cost(us):
    return pl.CostEstimate(flops=int(us * 1.15e7), bytes_accessed=1 << 12, transcendentals=0)


def limit(mib):
    return pltpu.CompilerParams(vmem_limit_bytes=mib * 1024 * 1024)


SMEM = pl.BlockSpec(memory_space=pltpu.SMEM)
ANYWHERE = pl.BlockSpec(memory_space=pl.ANY)
TOKEN = jax.ShapeDtypeStruct((SUB, LANES), f32)
TOKEN_SPEC = whole((SUB, LANES))
ROWS = (20, WT, SUB, LANES)


def gather_kernel(info, x_hbm, out_ref, edge_ref, flat, sems):
    octet = pl.program_id(0)
    first = pl.multiple_of(octet * 16 * SUB, 16 * SUB)
    copies = [
        pltpu.make_async_copy(
            x_hbm.at[pl.ds(first, 16 * SUB), t * LANES : (t + 1) * LANES], flat.at[t], sems.at[t]
        )
        for t in range(WT)
    ]
    for copy in copies:
        copy.start()
    for copy in copies:
        copy.wait()
    for r in range(16):
        for t in range(WT):
            out_ref[0, r + 2, t] = flat[t, pl.ds(r, SUB, stride=16), :]
    top = 14 * (1 - info[3])
    for r in range(2):
        for t in range(WT):
            edge_ref[0, r, t] = flat[t, pl.ds(top + r, SUB, stride=16), :]


def gather_rows(x, info):
    return pl.pallas_call(
        gather_kernel,
        out_shape=[jax.ShapeDtypeStruct((2, n) + ROWS[1:], f32) for n in (20, 2)],
        grid=(2,),
        in_specs=[SMEM, ANYWHERE],
        out_specs=[pl.BlockSpec((1, n) + ROWS[1:], lambda o: (o, 0, 0, 0, 0)) for n in (20, 2)],
        scratch_shapes=[pltpu.VMEM((WT, 16 * SUB, LANES), f32), pltpu.SemaphoreType.DMA((WT,))],
        compiler_params=limit(16),
        cost_estimate=cost(3.0),
        name="gather_rows",
    )(info, x)


def filter_kernel(octet, other, info, taps_ref, _, halo_ref, *rest):
    rows, outs, token, weight = rest[-7], rest[-6:-2], rest[-2], rest[-1]
    step = pl.program_id(0)
    xs = rows.at[octet + step]
    for r in range(2):
        for t in range(WT):
            if other:
                value = halo_ref[r, :, t * LANES : (t + 1) * LANES]
            else:
                value = halo_ref[0, r, t]
            xs[r, t] = value
            xs[18 + r, t] = value
    taps = [taps_ref[i, j] for i in range(5) for j in range(5)]
    overlap = info[0].astype(f32)
    lane = lane_index().astype(f32) + 0.5
    for t in range(WT):
        weight[t] = jnp.minimum((lane + t * LANES) / overlap, 1.0)
    token[...] = jnp.zeros_like(token)
    x_of = 1 - info[3] if other else info[3]
    for s in range(4):

        @pl.loop(0, 2)
        def _(c):
            def store(t, value):
                outs[s][step, c, t] = value

            r = lax.rem(info[2] + s, 4) * 4 + x_of * 2 + c
            filter_row(taps, weight, xs, r, store)


def phase_filter(xt, halo, taps, info, octet, count, other, deps=()):
    tile = (WT, SUB, LANES)
    if other:
        halo_spec = pl.BlockSpec((2, SUB, W), lambda o: (0, octet + o, 0))
    else:
        halo_spec = pl.BlockSpec((1, 2) + tile, lambda o: (octet + o, 0, 0, 0, 0))
    local = pl.BlockSpec(memory_space=pltpu.VMEM)
    return pl.pallas_call(
        functools.partial(filter_kernel, octet, other),
        out_shape=[jax.ShapeDtypeStruct(xt.shape, f32)]
        + [jax.ShapeDtypeStruct((count, 2) + tile, f32)] * 4
        + [TOKEN],
        grid=(count,),
        in_specs=[SMEM, SMEM, local, halo_spec] + [ANYWHERE] * len(deps),
        out_specs=[local] * 5 + [TOKEN_SPEC],
        scratch_shapes=[pltpu.VMEM(tile, f32)],
        input_output_aliases={2: 0},
        compiler_params=limit(8),
        cost_estimate=cost(5.0),
        name="phase_filter",
    )(info, taps, xt, halo, *deps)


def stitch_kernel(by_core, info, r0, r1, r2, r3, *rest):
    outs, token = (rest[-3:-1] if by_core else rest[-2:-1]), rest[-1]
    token[...] = jnp.zeros_like(token)
    shift, y, core = W - info[0], info[2], info[4]
    for near, far, place_of in ((r0, r2, y), (r1, r3, lax.rem(y + 3, 4))):
        near_is_own = place_of < 2
        half = lax.rem(place_of, 2)
        for out, row in zip(outs, (core, 1 - core)):

            def put(t, v):
                out[half, 0, t] = v

            def add(t, v):
                out[half, 0, t] = out[half, 0, t] + v

            at = (0, row) if by_core else (0,)
            stitch(
                lambda t: jnp.where(near_is_own, near[*at, t], far[*at, t]),
                lambda t: jnp.where(near_is_own, far[*at, t], near[*at, t]),
                put,
                add,
                shift,
            )


def stitch_pairs(parts, info, deps=()):
    count, by_core = parts[0].shape[0], parts[0].ndim == 5
    block = (1,) + parts[0].shape[1:]
    outs = [jax.ShapeDtypeStruct((2, count, CT, SUB, LANES), f32)] * (2 if by_core else 1)
    return pl.pallas_call(
        functools.partial(stitch_kernel, by_core),
        out_shape=outs + [TOKEN],
        in_specs=[SMEM]
        + [pl.BlockSpec(block, lambda o: (o,) + (0,) * (len(block) - 1))] * 4
        + [ANYWHERE] * len(deps),
        out_specs=[pl.BlockSpec((2, 1, CT, SUB, LANES), lambda o: (0, o, 0, 0, 0))] * len(outs) + [TOKEN_SPEC],
        grid=(count,),
        compiler_params=limit(8),
        cost_estimate=cost(1.5),
        name="stitch_pairs",
    )(info, *parts, *deps)


SLOTS = 5


def ramp_kernel(sources, info, *refs):
    rows, (tw_ref, gain_ref, fh, fl, gh, gl) = refs[:sources], refs[sources : sources + 6]
    out_ref, token, (sig, mid, spec) = refs[-5], refs[-4], refs[-3:]
    token[...] = jnp.zeros_like(token)
    steps = [(source, which) for source in rows for which in range(source.shape[1])]
    for n, (source, which) in enumerate(steps):

        @pl.when(pl.program_id(0) == n)
        def _():
            for half in range(2):
                place(lambda t: source[half, which, t], sig, half, info[1])

    def write(half, n, value):
        out_ref[half, 0, 0, 0, :, n * LANES : (n + 1) * LANES] = value

    ramp(sig, mid, spec, tw_ref, gain_ref, fh, fl, gh, gl, write)


def constants():
    twiddle, gain, forward = tables()
    fh, fl = split(forward)
    gh, gl = split(forward.T.copy())
    return [jnp.asarray(v) for v in (twiddle, gain, fh, fl, gh, gl)]


def ramp_filter(rows, info, consts, slot, result=None, deps=()):
    steps = sum(v.shape[1] for v in rows)
    local = pl.BlockSpec(memory_space=pltpu.VMEM)
    in_specs = [local] * (len(rows) + len(consts)) + [ANYWHERE] * len(deps)
    operands = [*rows, *consts, *deps]
    alias = {}
    if result is not None:
        alias = {1 + len(operands): 0}
        in_specs.append(ANYWHERE)
        operands.append(result)

    def target(i, info):
        at = SLOTS + 3 * (slot + i)
        return (0, info[at], info[at + 1], info[at + 2], 0, 0)

    return pl.pallas_call(
        functools.partial(ramp_kernel, len(rows)),
        out_shape=[jax.ShapeDtypeStruct((2, 2, 2, 2, SUB, S), f32), TOKEN],
        grid_spec=pltpu.PrefetchScalarGridSpec(
            num_scalar_prefetch=1,
            grid=(steps,),
            in_specs=in_specs,
            out_specs=[pl.BlockSpec((2, 1, 1, 1, SUB, S), target), whole((SUB, LANES))],
            scratch_shapes=[
                pltpu.VMEM((2, ST + 2, SUB, LANES), f32),
                pltpu.VMEM((2, 64, SUB, LANES), f32),
                pltpu.VMEM((64 * SUB, 2 * LANES), f32),
            ],
        ),
        input_output_aliases=alias,
        compiler_params=limit(16),
        cost_estimate=cost(2.0),
        name="ramp_filter",
    )(info, *operands)


def y_step(block, s):
    route = [(i, (i // 4 + s) % 4 * 4 + i % 4) for i in range(16)]
    return lax.ppermute(block, "ang", route)


def flip(block, bits):
    return lax.ppermute(block, "ang", [(i, i ^ bits) for i in range(16)])


def row_step(block, up_side):
    rows, angs = lax.axis_size("row"), lax.axis_size("ang")
    route = []
    for r in range(rows):
        for a in range(angs):
            to = r + 1 if a // 2 % 2 == up_side else r - 1
            if 0 <= to < rows:
                route.append((a * rows + r, a * rows + to))
    return lax.ppermute(block, ("ang", "row"), route)


def shards(projections, phase_kernel, correlation, offset):
    me = lax.axis_index("ang").astype(jnp.uint32)
    y, x, core = [v.astype(jnp.int32) for v in (me >> 2, (me >> 1) & 1, me & 1)]
    slots = []
    for x_of, core_of, octet in (
        (1 - x, core, 0),
        (1 - x, 1 - core, 0),
        (1 - x, core, 1),
        (1 - x, 1 - core, 1),
        (x, core, 0),
        (x, core, 1),
        (x, 1 - core, 0),
        (x, 1 - core, 1),
    ):
        slots += [x_of, core_of, jnp.int32(octet)]
    info = jnp.stack([correlation[0], offset[0], y, x, core] + slots)
    consts = constants()

    def y_exchange(parts):
        return [parts[0]] + [y_step(parts[s], s) for s in (1, 2, 3)]

    def send(rows):
        return flip(rows[0], 2), flip(rows[1], 3)

    edge = lax.dynamic_slice(projections, (0, 14 * x, 0), (16, 2, W))
    near = [row_step(jnp.swapaxes(edge, 0, 1), 1)] * 2
    xt, edges = gather_rows(projections.reshape(256, W), info)
    far = row_step(edges, 0)
    xt, *sent_0, done = phase_filter(xt, near[0], phase_kernel, info, 0, 1, True)
    parts_0 = y_exchange(sent_0)
    xt, *sent_1, done = phase_filter(xt, near[1], phase_kernel, info, 1, 1, True, [done])
    parts_1 = y_exchange(sent_1)
    *rows_0, done = stitch_pairs(parts_0, info, [done])
    arrived_0 = send(rows_0)
    xt, *sent_2, done = phase_filter(xt, far, phase_kernel, info, 0, 2, False, [done])
    parts_2 = y_exchange(sent_2)
    *rows_1, done = stitch_pairs(parts_1, info, [done])
    arrived_1 = send(rows_1)
    result, done = ramp_filter(arrived_0, info, consts, 0, None, [done])
    result, done = ramp_filter(arrived_1, info, consts, 2, result)
    *rows_2, done = stitch_pairs(parts_2, info, [done])
    swapped = flip(rows_2[1], 1)
    result, done = ramp_filter([rows_2[0]], info, consts, 4, result)
    result, done = ramp_filter([swapped], info, consts, 6, result)
    return result.reshape(1, 128, S)


def solution(mesh):
    return jax.shard_map(
        shards,
        mesh=mesh,
        in_specs=(P("ang", "row", None), P(), P(), P()),
        out_specs=P(("row", "ang"), None, None),
        check_vma=False,
    )
```

```python
import functools
import math

import jax
import jax.numpy as jnp
import numpy as np
from jax import lax
from jax.experimental import pallas as pl
from jax.experimental.pallas import tpu as pltpu
from jax.sharding import PartitionSpec as P

W = 4608
S = 8192
LANES = 128
SUB = 8
WT = W // LANES
ST = S // LANES
CT = 61

f32 = jnp.float32
bf16 = jnp.bfloat16


def tables():
    k1 = np.arange(64)
    n2 = np.arange(128)
    turn = 2 * np.pi * (k1[:, None] * n2[None, :]) / S
    twiddle = np.stack([np.cos(turn), -np.sin(turn)])
    twiddle = np.repeat(twiddle[:, :, None, :], SUB, axis=2).astype(np.float32)
    freq = k1[:, None] + 64 * n2[None, :]
    gain = 2.0 * np.minimum(freq, S - freq) / S / S
    gain = np.repeat(gain[:, None, :], SUB, axis=1).reshape(64 * SUB, 128).astype(np.float32)
    angle = 2 * np.pi * ((n2[:, None] * n2[None, :]) % 128) / 128
    c, s = np.cos(angle), np.sin(angle)
    forward = np.block([[c, -s], [s, c]]).astype(np.float32)
    return twiddle, gain, forward


def split(matrix):
    high = matrix.astype(jnp.bfloat16)
    low = (matrix - high.astype(np.float32)).astype(jnp.bfloat16)
    return high, low


def cadd(a, b):
    return (a[0] + b[0], a[1] + b[1])


def csub(a, b):
    return (a[0] - b[0], a[1] - b[1])


def turn_quarter(a, sign):
    return (-a[1], a[0]) if sign > 0 else (a[1], -a[0])


def dft4(x0, x1, x2, x3, sign):
    a0, a1 = cadd(x0, x2), csub(x0, x2)
    a2, a3 = cadd(x1, x3), turn_quarter(csub(x1, x3), sign)
    return cadd(a0, a2), cadd(a1, a3), csub(a0, a2), csub(a1, a3)


def dft8(x, sign):
    e = dft4(x[0], x[2], x[4], x[6], sign)
    o = dft4(x[1], x[3], x[5], x[7], sign)
    h = math.sqrt(0.5)
    r, m = o[1]
    o1 = ((r - m) * h, (m + r) * h) if sign > 0 else ((r + m) * h, (m - r) * h)
    o2 = turn_quarter(o[2], sign)
    r, m = o[3]
    o3 = ((r + m) * -h, (r - m) * h) if sign > 0 else ((m - r) * h, (r + m) * -h)
    odd = (o[0], o1, o2, o3)
    return [cadd(e[k], odd[k]) for k in range(4)] + [csub(e[k], odd[k]) for k in range(4)]


def const_turn(a, count, sign):
    count %= 64
    if count == 0:
        return a
    c = math.cos(2 * math.pi * count / 64)
    s = sign * math.sin(2 * math.pi * count / 64)
    return (a[0] * c - a[1] * s, a[0] * s + a[1] * c)


def lane_index():
    return lax.broadcasted_iota(jnp.int32, (SUB, LANES), 1)


def filter_row(taps, w_ref, xs, r, store):
    lane = lane_index()
    zero = jnp.zeros((SUB, LANES), f32)
    r0, r1, left, right3, right4 = zero, zero, None, None, None
    for t in range(WT + 1):
        if t < WT:
            rows = [xs[r + i, t] for i in range(5)]
            acc = []
            for j in range(5):
                total = taps[j] * rows[0]
                for i in range(1, 5):
                    total = total + taps[5 * i + j] * rows[i]
                acc.append(total)
            n0, n1 = pltpu.roll(acc[0], 2, 1), pltpu.roll(acc[1], 1, 1)
            n3, n4 = pltpu.roll(acc[3], LANES - 1, 1), pltpu.roll(acc[4], LANES - 2, 1)
        else:
            n3 = n4 = zero
        if t > 0:
            value = left + jnp.where(lane < LANES - 1, right3, n3) + jnp.where(lane < LANES - 2, right4, n4)
            store(t - 1, value * w_ref[t - 1])
        if t < WT:
            left = acc[2] + jnp.where(lane >= 2, n0, r0) + jnp.where(lane >= 1, n1, r1)
            r0, r1, right3, right4 = n0, n1, n3, n4


def stitch(own, opp, put, add, shift):
    lane = lane_index()
    backwards = LANES - 1 - lane
    zero = jnp.zeros((SUB, LANES), f32)
    for t in range(CT):
        put(t, jnp.take_along_axis(opp(WT - 1 - t), backwards, axis=1) if t < WT else zero)
    whole, part = shift // LANES, lax.rem(shift, LANES)
    before = zero
    for t in range(WT + 1):
        now = pltpu.roll(own(t), part, 1) if t < WT else zero
        add(whole + t, jnp.where(lane >= part, now, before))
        before = now


def place(source, sig, side, shift):
    lane = lane_index()
    zero = jnp.zeros((SUB, LANES), f32)
    whole, part = shift // LANES, lax.rem(shift, LANES)
    for t in range(4):
        sig[side, t] = zero
        sig[side, ST - 4 + t] = zero
    before = zero
    for t in range(CT + 1):
        now = pltpu.roll(source(t), part, 1) if t < CT else zero
        sig[side, whole + t] = jnp.where(lane >= part, now, before)
        before = now


def matmul3(x, high, low):
    xh = x.astype(bf16)
    xl = (x - xh.astype(f32)).astype(bf16)
    dot = functools.partial(jnp.dot, preferred_element_type=f32)
    return dot(xh, low) + dot(xl, high) + dot(xh, high)


def ramp(sig, mid, spec, tw_ref, gain_ref, fh, fl, gh, gl, put):
    for b in range(8):
        x = dft8([(sig[0, 8 * a + b], sig[1, 8 * a + b]) for a in range(8)], -1)
        for c in range(8):
            mid[0, 8 * b + c], mid[1, 8 * b + c] = const_turn(x[c], b * c, -1)
    for c in range(8):
        y = dft8([(mid[0, 8 * b + c], mid[1, 8 * b + c]) for b in range(8)], -1)
        for d in range(8):
            k = c + 8 * d
            tr, ti = tw_ref[0, k], tw_ref[1, k]
            re, im = y[d]
            spec[k * SUB : (k + 1) * SUB, :LANES] = re * tr - im * ti
            spec[k * SUB : (k + 1) * SUB, LANES:] = re * ti + im * tr
    step = 128
    for m in range(0, 64 * SUB, step):
        z = matmul3(spec[m : m + step, :], fh[...], fl[...])
        g = gain_ref[m : m + step, :]
        z = z * jnp.concatenate([g, g], axis=1)
        spec[m : m + step, :] = matmul3(z, gh[...], gl[...])
    for c in range(8):
        y = []
        for d in range(8):
            k = c + 8 * d
            tr, ti = tw_ref[0, k], tw_ref[1, k]
            re, im = spec[k * SUB : (k + 1) * SUB, :LANES], spec[k * SUB : (k + 1) * SUB, LANES:]
            y.append((re * tr + im * ti, im * tr - re * ti))
        v = dft8(y, 1)
        for b in range(8):
            mid[0, 8 * b + c], mid[1, 8 * b + c] = const_turn(v[b], b * c, 1)
    for b in range(8):
        s = dft8([(mid[0, 8 * b + c], mid[1, 8 * b + c]) for c in range(8)], 1)
        for a in range(8):
            put(0, 8 * a + b, s[a][0])
            put(1, 8 * a + b, s[a][1])


def whole(shape):
    return pl.BlockSpec(shape, lambda *_: (0,) * len(shape))


def cost(us):
    return pl.CostEstimate(flops=int(us * 1.15e7), bytes_accessed=1 << 12, transcendentals=0)


def limit(mib):
    return pltpu.CompilerParams(vmem_limit_bytes=mib * 1024 * 1024)


SMEM = pl.BlockSpec(memory_space=pltpu.SMEM)
ANYWHERE = pl.BlockSpec(memory_space=pl.ANY)
TOKEN = jax.ShapeDtypeStruct((SUB, LANES), f32)
TOKEN_SPEC = whole((SUB, LANES))
ROWS = (20, WT, SUB, LANES)


def gather_kernel(x_hbm, out_ref, flat, sems):
    octet = pl.program_id(0)
    first = pl.multiple_of(octet * 16 * SUB, 16 * SUB)
    copies = [
        pltpu.make_async_copy(
            x_hbm.at[pl.ds(first, 16 * SUB), t * LANES : (t + 1) * LANES], flat.at[t], sems.at[t]
        )
        for t in range(WT)
    ]
    for copy in copies:
        copy.start()
    for copy in copies:
        copy.wait()
    for r in range(16):
        for t in range(WT):
            out_ref[0, r + 2, t] = flat[t, pl.ds(r, SUB, stride=16), :]


def gather_rows(x):
    return pl.pallas_call(
        gather_kernel,
        out_shape=jax.ShapeDtypeStruct((2,) + ROWS, f32),
        grid=(2,),
        in_specs=[ANYWHERE],
        out_specs=pl.BlockSpec((1,) + ROWS, lambda o: (o, 0, 0, 0, 0)),
        scratch_shapes=[pltpu.VMEM((WT, 16 * SUB, LANES), f32), pltpu.SemaphoreType.DMA((WT,))],
        compiler_params=limit(16),
        cost_estimate=cost(3.0),
        name="gather_rows",
    )(x)


def filter_kernel(octet, other, edge_octets, info, taps_ref, _, halo_ref, *rest):
    rows, outs, edges, token, weight = rest[-8], rest[-7:-3], rest[-3], rest[-2], rest[-1]
    step = pl.program_id(0)
    xs = rows.at[octet + step]
    for r in range(2):
        for t in range(WT):
            if other:
                value = halo_ref[r, :, t * LANES : (t + 1) * LANES]
            else:
                value = halo_ref[0, r, t]
            xs[r, t] = value
            xs[18 + r, t] = value
    top = 2 + 14 * (1 - info[3])
    for n, edge_octet in enumerate(edge_octets):
        for r in range(2):
            for t in range(WT):
                edges[n, r, t] = rows[edge_octet, top + r, t]
    taps = [taps_ref[i, j] for i in range(5) for j in range(5)]
    overlap = info[0].astype(f32)
    lane = lane_index().astype(f32) + 0.5
    for t in range(WT):
        weight[t] = jnp.minimum((lane + t * LANES) / overlap, 1.0)
    token[...] = jnp.zeros_like(token)
    x_of = 1 - info[3] if other else info[3]
    for s in range(4):

        @pl.loop(0, 2)
        def _(c):
            def store(t, value):
                outs[s][step, c, t] = value

            r = lax.rem(info[2] + s, 4) * 4 + x_of * 2 + c
            filter_row(taps, weight, xs, r, store)


def phase_filter(xt, halo, taps, info, octet, count, other, deps=(), edge_octets=()):
    tile = (WT, SUB, LANES)
    if other:
        halo_spec = pl.BlockSpec((2, SUB, W), lambda o: (0, octet + o, 0))
    else:
        halo_spec = pl.BlockSpec((1, 2) + tile, lambda o: (octet + o, 0, 0, 0, 0))
    local = pl.BlockSpec(memory_space=pltpu.VMEM)
    return pl.pallas_call(
        functools.partial(filter_kernel, octet, other, edge_octets),
        out_shape=[jax.ShapeDtypeStruct(xt.shape, f32)]
        + [jax.ShapeDtypeStruct((count, 2) + tile, f32)] * 4
        + [jax.ShapeDtypeStruct((max(len(edge_octets), 1), 2) + tile, f32), TOKEN],
        grid=(count,),
        in_specs=[SMEM, SMEM, local, halo_spec] + [ANYWHERE] * len(deps),
        out_specs=[local] * 6 + [TOKEN_SPEC],
        scratch_shapes=[pltpu.VMEM(tile, f32)],
        input_output_aliases={2: 0},
        compiler_params=limit(8),
        cost_estimate=cost(5.0),
        name="phase_filter",
    )(info, taps, xt, halo, *deps)


def stitch_kernel(by_core, info, r0, r1, r2, r3, *rest):
    outs, token = (rest[-3:-1] if by_core else rest[-2:-1]), rest[-1]
    token[...] = jnp.zeros_like(token)
    shift, y, core = W - info[0], info[2], info[4]
    for near, far, place_of in ((r0, r2, y), (r1, r3, lax.rem(y + 3, 4))):
        near_is_own = place_of < 2
        half = lax.rem(place_of, 2)
        for out, row in zip(outs, (core, 1 - core)):

            def put(t, v):
                out[half, 0, t] = v

            def add(t, v):
                out[half, 0, t] = out[half, 0, t] + v

            at = (0, row) if by_core else (0,)
            stitch(
                lambda t: jnp.where(near_is_own, near[*at, t], far[*at, t]),
                lambda t: jnp.where(near_is_own, far[*at, t], near[*at, t]),
                put,
                add,
                shift,
            )


def stitch_pairs(parts, info, deps=()):
    count, by_core = parts[0].shape[0], parts[0].ndim == 5
    block = (1,) + parts[0].shape[1:]
    outs = [jax.ShapeDtypeStruct((2, count, CT, SUB, LANES), f32)] * (2 if by_core else 1)
    return pl.pallas_call(
        functools.partial(stitch_kernel, by_core),
        out_shape=outs + [TOKEN],
        in_specs=[SMEM]
        + [pl.BlockSpec(block, lambda o: (o,) + (0,) * (len(block) - 1))] * 4
        + [ANYWHERE] * len(deps),
        out_specs=[pl.BlockSpec((2, 1, CT, SUB, LANES), lambda o: (0, o, 0, 0, 0))] * len(outs) + [TOKEN_SPEC],
        grid=(count,),
        compiler_params=limit(8),
        cost_estimate=cost(1.5),
        name="stitch_pairs",
    )(info, *parts, *deps)


SLOTS = 5


def ramp_kernel(sources, info, *refs):
    rows, (tw_ref, gain_ref, fh, fl, gh, gl) = refs[:sources], refs[sources : sources + 6]
    out_ref, token, (sig, mid, spec) = refs[-5], refs[-4], refs[-3:]
    token[...] = jnp.zeros_like(token)
    steps = [(source, which) for source in rows for which in range(source.shape[1])]
    for n, (source, which) in enumerate(steps):

        @pl.when(pl.program_id(0) == n)
        def _():
            for half in range(2):
                place(lambda t: source[half, which, t], sig, half, info[1])

    def write(half, n, value):
        out_ref[half, 0, 0, 0, :, n * LANES : (n + 1) * LANES] = value

    ramp(sig, mid, spec, tw_ref, gain_ref, fh, fl, gh, gl, write)


def constants():
    twiddle, gain, forward = tables()
    fh, fl = split(forward)
    gh, gl = split(forward.T.copy())
    return [jnp.asarray(v) for v in (twiddle, gain, fh, fl, gh, gl)]


def ramp_filter(rows, info, consts, slot, result=None, deps=()):
    steps = sum(v.shape[1] for v in rows)
    local = pl.BlockSpec(memory_space=pltpu.VMEM)
    in_specs = [local] * (len(rows) + len(consts)) + [ANYWHERE] * len(deps)
    operands = [*rows, *consts, *deps]
    alias = {}
    if result is not None:
        alias = {1 + len(operands): 0}
        in_specs.append(ANYWHERE)
        operands.append(result)

    def target(i, info):
        at = SLOTS + 3 * (slot + i)
        return (0, info[at], info[at + 1], info[at + 2], 0, 0)

    return pl.pallas_call(
        functools.partial(ramp_kernel, len(rows)),
        out_shape=[jax.ShapeDtypeStruct((2, 2, 2, 2, SUB, S), f32), TOKEN],
        grid_spec=pltpu.PrefetchScalarGridSpec(
            num_scalar_prefetch=1,
            grid=(steps,),
            in_specs=in_specs,
            out_specs=[pl.BlockSpec((2, 1, 1, 1, SUB, S), target), whole((SUB, LANES))],
            scratch_shapes=[
                pltpu.VMEM((2, ST + 2, SUB, LANES), f32),
                pltpu.VMEM((2, 64, SUB, LANES), f32),
                pltpu.VMEM((64 * SUB, 2 * LANES), f32),
            ],
        ),
        input_output_aliases=alias,
        compiler_params=limit(16),
        cost_estimate=cost(2.0),
        name="ramp_filter",
    )(info, *operands)


def y_step(block, s):
    route = [(i, (i // 4 + s) % 4 * 4 + i % 4) for i in range(16)]
    return lax.ppermute(block, "ang", route)


def flip(block, bits):
    return lax.ppermute(block, "ang", [(i, i ^ bits) for i in range(16)])


def row_step(block, up_side):
    rows, angs = lax.axis_size("row"), lax.axis_size("ang")
    route = []
    for r in range(rows):
        for a in range(angs):
            to = r + 1 if a // 2 % 2 == up_side else r - 1
            if 0 <= to < rows:
                route.append((a * rows + r, a * rows + to))
    return lax.ppermute(block, ("ang", "row"), route)


def shards(projections, phase_kernel, correlation, offset):
    me = lax.axis_index("ang").astype(jnp.uint32)
    y, x, core = [v.astype(jnp.int32) for v in (me >> 2, (me >> 1) & 1, me & 1)]
    slots = []
    for x_of, core_of, octet in (
        (1 - x, core, 0),
        (1 - x, 1 - core, 0),
        (1 - x, core, 1),
        (1 - x, 1 - core, 1),
        (x, core, 0),
        (x, core, 1),
        (x, 1 - core, 0),
        (x, 1 - core, 1),
    ):
        slots += [x_of, core_of, jnp.int32(octet)]
    info = jnp.stack([correlation[0], offset[0], y, x, core] + slots)
    consts = constants()

    def y_exchange(parts):
        return [parts[0]] + [y_step(parts[s], s) for s in (1, 2, 3)]

    def send(rows):
        return flip(rows[0], 2), flip(rows[1], 3)

    edge = lax.dynamic_slice(projections, (0, 14 * x, 0), (16, 2, W))
    near = [row_step(jnp.swapaxes(edge, 0, 1), 1)] * 2
    xt = gather_rows(projections.reshape(256, W))
    xt, *sent_0, edges_0, done = phase_filter(xt, near[0], phase_kernel, info, 0, 1, True, [], (0, 1))
    far = row_step(edges_0, 0)
    parts_0 = y_exchange(sent_0)
    xt, *sent_1, edges_1, done = phase_filter(xt, near[1], phase_kernel, info, 1, 1, True, [done], ())
    parts_1 = y_exchange(sent_1)
    *rows_0, done = stitch_pairs(parts_0, info, [done])
    arrived_0 = send(rows_0)
    xt, *sent_2, _, done = phase_filter(xt, far, phase_kernel, info, 0, 2, False, [done])
    parts_2 = y_exchange(sent_2)
    *rows_1, done = stitch_pairs(parts_1, info, [done])
    arrived_1 = send(rows_1)
    result, done = ramp_filter(arrived_0, info, consts, 0, None, [done])
    *rows_2, done = stitch_pairs(parts_2, info, [done, arrived_1[0][0, 0, 0], arrived_1[1][0, 0, 0]])
    swapped = flip(rows_2[1], 1)
    result, done = ramp_filter([*arrived_1, rows_2[0]], info, consts, 2, result)
    result, done = ramp_filter([swapped], info, consts, 6, result)
    return result.reshape(1, 128, S)


def solution(mesh):
    return jax.shard_map(
        shards,
        mesh=mesh,
        in_specs=(P("ang", "row", None), P(), P(), P()),
        out_specs=P(("row", "ang"), None, None),
        check_vma=False,
    )
```

```python
import functools
import math

import jax
import jax.numpy as jnp
import numpy as np
from jax import lax
from jax.experimental import pallas as pl
from jax.experimental.pallas import tpu as pltpu
from jax.sharding import PartitionSpec as P

W = 4608
S = 8192
LANES = 128
SUB = 8
WT = W // LANES
ST = S // LANES
CT = 61

f32 = jnp.float32
bf16 = jnp.bfloat16


def tables():
    k1 = np.arange(64)
    n2 = np.arange(128)
    turn = 2 * np.pi * (k1[:, None] * n2[None, :]) / S
    twiddle = np.stack([np.cos(turn), -np.sin(turn)])
    twiddle = np.repeat(twiddle[:, :, None, :], SUB, axis=2).astype(np.float32)
    freq = k1[:, None] + 64 * n2[None, :]
    gain = 2.0 * np.minimum(freq, S - freq) / S / S
    gain = np.repeat(gain[:, None, :], SUB, axis=1).reshape(64 * SUB, 128).astype(np.float32)
    angle = 2 * np.pi * ((n2[:, None] * n2[None, :]) % 128) / 128
    c, s = np.cos(angle), np.sin(angle)
    forward = np.block([[c, -s], [s, c]]).astype(np.float32)
    return twiddle, gain, forward


def split(matrix):
    high = matrix.astype(jnp.bfloat16)
    low = (matrix - high.astype(np.float32)).astype(jnp.bfloat16)
    return high, low


def cadd(a, b):
    return (a[0] + b[0], a[1] + b[1])


def csub(a, b):
    return (a[0] - b[0], a[1] - b[1])


def turn_quarter(a, sign):
    return (-a[1], a[0]) if sign > 0 else (a[1], -a[0])


def dft4(x0, x1, x2, x3, sign):
    a0, a1 = cadd(x0, x2), csub(x0, x2)
    a2, a3 = cadd(x1, x3), turn_quarter(csub(x1, x3), sign)
    return cadd(a0, a2), cadd(a1, a3), csub(a0, a2), csub(a1, a3)


def dft8(x, sign):
    e = dft4(x[0], x[2], x[4], x[6], sign)
    o = dft4(x[1], x[3], x[5], x[7], sign)
    h = math.sqrt(0.5)
    r, m = o[1]
    o1 = ((r - m) * h, (m + r) * h) if sign > 0 else ((r + m) * h, (m - r) * h)
    o2 = turn_quarter(o[2], sign)
    r, m = o[3]
    o3 = ((r + m) * -h, (r - m) * h) if sign > 0 else ((m - r) * h, (r + m) * -h)
    odd = (o[0], o1, o2, o3)
    return [cadd(e[k], odd[k]) for k in range(4)] + [csub(e[k], odd[k]) for k in range(4)]


def const_turn(a, count, sign):
    count %= 64
    if count == 0:
        return a
    c = math.cos(2 * math.pi * count / 64)
    s = sign * math.sin(2 * math.pi * count / 64)
    return (a[0] * c - a[1] * s, a[0] * s + a[1] * c)


def lane_index():
    return lax.broadcasted_iota(jnp.int32, (SUB, LANES), 1)


def filter_row(taps, w_ref, xs, r, store):
    lane = lane_index()
    zero = jnp.zeros((SUB, LANES), f32)
    r0, r1, left, right3, right4 = zero, zero, None, None, None
    for t in range(WT + 1):
        if t < WT:
            rows = [xs[r + i, t] for i in range(5)]
            acc = []
            for j in range(5):
                total = taps[j] * rows[0]
                for i in range(1, 5):
                    total = total + taps[5 * i + j] * rows[i]
                acc.append(total)
            n0, n1 = pltpu.roll(acc[0], 2, 1), pltpu.roll(acc[1], 1, 1)
            n3, n4 = pltpu.roll(acc[3], LANES - 1, 1), pltpu.roll(acc[4], LANES - 2, 1)
        else:
            n3 = n4 = zero
        if t > 0:
            value = left + jnp.where(lane < LANES - 1, right3, n3) + jnp.where(lane < LANES - 2, right4, n4)
            store(t - 1, value * w_ref[t - 1])
        if t < WT:
            left = acc[2] + jnp.where(lane >= 2, n0, r0) + jnp.where(lane >= 1, n1, r1)
            r0, r1, right3, right4 = n0, n1, n3, n4


def stitch(own, opp, put, add, shift):
    lane = lane_index()
    backwards = LANES - 1 - lane
    zero = jnp.zeros((SUB, LANES), f32)
    for t in range(CT):
        put(t, jnp.take_along_axis(opp(WT - 1 - t), backwards, axis=1) if t < WT else zero)
    whole, part = shift // LANES, lax.rem(shift, LANES)
    before = zero
    for t in range(WT + 1):
        now = pltpu.roll(own(t), part, 1) if t < WT else zero
        add(whole + t, jnp.where(lane >= part, now, before))
        before = now


def place(source, sig, side, shift):
    lane = lane_index()
    zero = jnp.zeros((SUB, LANES), f32)
    whole, part = shift // LANES, lax.rem(shift, LANES)
    for t in range(4):
        sig[side, t] = zero
        sig[side, ST - 4 + t] = zero
    before = zero
    for t in range(CT + 1):
        now = pltpu.roll(source(t), part, 1) if t < CT else zero
        sig[side, whole + t] = jnp.where(lane >= part, now, before)
        before = now


def matmul3(x, high, low):
    xh = x.astype(bf16)
    xl = (x - xh.astype(f32)).astype(bf16)
    dot = functools.partial(jnp.dot, preferred_element_type=f32)
    return dot(xh, low) + dot(xl, high) + dot(xh, high)


def ramp(sig, mid, spec, tw_ref, gain_ref, fh, fl, gh, gl, put):
    for b in range(8):
        x = dft8([(sig[0, 8 * a + b], sig[1, 8 * a + b]) for a in range(8)], -1)
        for c in range(8):
            mid[0, 8 * b + c], mid[1, 8 * b + c] = const_turn(x[c], b * c, -1)
    for c in range(8):
        y = dft8([(mid[0, 8 * b + c], mid[1, 8 * b + c]) for b in range(8)], -1)
        for d in range(8):
            k = c + 8 * d
            tr, ti = tw_ref[0, k], tw_ref[1, k]
            re, im = y[d]
            spec[k * SUB : (k + 1) * SUB, :LANES] = re * tr - im * ti
            spec[k * SUB : (k + 1) * SUB, LANES:] = re * ti + im * tr
    step = 128
    for m in range(0, 64 * SUB, step):
        z = matmul3(spec[m : m + step, :], fh[...], fl[...])
        g = gain_ref[m : m + step, :]
        z = z * jnp.concatenate([g, g], axis=1)
        spec[m : m + step, :] = matmul3(z, gh[...], gl[...])
    for c in range(8):
        y = []
        for d in range(8):
            k = c + 8 * d
            tr, ti = tw_ref[0, k], tw_ref[1, k]
            re, im = spec[k * SUB : (k + 1) * SUB, :LANES], spec[k * SUB : (k + 1) * SUB, LANES:]
            y.append((re * tr + im * ti, im * tr - re * ti))
        v = dft8(y, 1)
        for b in range(8):
            mid[0, 8 * b + c], mid[1, 8 * b + c] = const_turn(v[b], b * c, 1)
    for b in range(8):
        s = dft8([(mid[0, 8 * b + c], mid[1, 8 * b + c]) for c in range(8)], 1)
        for a in range(8):
            put(0, 8 * a + b, s[a][0])
            put(1, 8 * a + b, s[a][1])


def whole(shape):
    return pl.BlockSpec(shape, lambda *_: (0,) * len(shape))


def cost(us):
    return pl.CostEstimate(flops=int(us * 1.15e7), bytes_accessed=1 << 12, transcendentals=0)


def limit(mib):
    return pltpu.CompilerParams(vmem_limit_bytes=mib * 1024 * 1024)


SMEM = pl.BlockSpec(memory_space=pltpu.SMEM)
ANYWHERE = pl.BlockSpec(memory_space=pl.ANY)
TOKEN = jax.ShapeDtypeStruct((SUB, LANES), f32)
TOKEN_SPEC = whole((SUB, LANES))
ROWS = (20, WT, SUB, LANES)


def gather_kernel(x_hbm, out_ref, flat, sems):
    octet = pl.program_id(0)
    first = pl.multiple_of(octet * 16 * SUB, 16 * SUB)
    copies = [
        pltpu.make_async_copy(
            x_hbm.at[pl.ds(first, 16 * SUB), t * LANES : (t + 1) * LANES], flat.at[t], sems.at[t]
        )
        for t in range(WT)
    ]
    for copy in copies:
        copy.start()
    for copy in copies:
        copy.wait()
    for r in range(16):
        for t in range(WT):
            out_ref[0, r + 2, t] = flat[t, pl.ds(r, SUB, stride=16), :]


def gather_rows(x):
    return pl.pallas_call(
        gather_kernel,
        out_shape=jax.ShapeDtypeStruct((2,) + ROWS, f32),
        grid=(2,),
        in_specs=[ANYWHERE],
        out_specs=pl.BlockSpec((1,) + ROWS, lambda o: (o, 0, 0, 0, 0)),
        scratch_shapes=[pltpu.VMEM((WT, 16 * SUB, LANES), f32), pltpu.SemaphoreType.DMA((WT,))],
        compiler_params=limit(16),
        cost_estimate=cost(3.0),
        name="gather_rows",
    )(x)


def filter_kernel(octet, other, edge_octets, info, taps_ref, _, halo_ref, *rest):
    rows, outs, edges, token, weight = rest[-8], rest[-7:-3], rest[-3], rest[-2], rest[-1]
    step = pl.program_id(0)
    xs = rows.at[octet + step]
    for r in range(2):
        for t in range(WT):
            if other:
                value = halo_ref[r, :, t * LANES : (t + 1) * LANES]
            else:
                value = halo_ref[0, r, t]
            xs[r, t] = value
            xs[18 + r, t] = value
    top = 2 + 14 * (1 - info[3])
    for n, edge_octet in enumerate(edge_octets):
        for r in range(2):
            for t in range(WT):
                edges[n, r, t] = rows[edge_octet, top + r, t]
    taps = [taps_ref[i, j] for i in range(5) for j in range(5)]
    overlap = info[0].astype(f32)
    lane = lane_index().astype(f32) + 0.5
    for t in range(WT):
        weight[t] = jnp.minimum((lane + t * LANES) / overlap, 1.0)
    token[...] = jnp.zeros_like(token)
    x_of = 1 - info[3] if other else info[3]
    for s in range(4):

        @pl.loop(0, 2)
        def _(c):
            def store(t, value):
                outs[s][step, c, t] = value

            r = lax.rem(info[2] + s, 4) * 4 + x_of * 2 + c
            filter_row(taps, weight, xs, r, store)


def phase_filter(xt, halo, taps, info, octet, count, other, deps=(), edge_octets=()):
    tile = (WT, SUB, LANES)
    if other:
        halo_spec = pl.BlockSpec((2, SUB, W), lambda o: (0, octet + o, 0))
    else:
        halo_spec = pl.BlockSpec((1, 2) + tile, lambda o: (octet + o, 0, 0, 0, 0))
    local = pl.BlockSpec(memory_space=pltpu.VMEM)
    return pl.pallas_call(
        functools.partial(filter_kernel, octet, other, edge_octets),
        out_shape=[jax.ShapeDtypeStruct(xt.shape, f32)]
        + [jax.ShapeDtypeStruct((count, 2) + tile, f32)] * 4
        + [jax.ShapeDtypeStruct((max(len(edge_octets), 1), 2) + tile, f32), TOKEN],
        grid=(count,),
        in_specs=[SMEM, SMEM, local, halo_spec] + [ANYWHERE] * len(deps),
        out_specs=[local] * 6 + [TOKEN_SPEC],
        scratch_shapes=[pltpu.VMEM(tile, f32)],
        input_output_aliases={2: 0},
        compiler_params=limit(8),
        cost_estimate=cost(5.0),
        name="phase_filter",
    )(info, taps, xt, halo, *deps)


def stitch_kernel(by_core, info, r0, r1, r2, r3, *rest):
    outs, token = (rest[-3:-1] if by_core else rest[-2:-1]), rest[-1]
    token[...] = jnp.zeros_like(token)
    shift, y, core = W - info[0], info[2], info[4]
    for near, far, place_of in ((r0, r2, y), (r1, r3, lax.rem(y + 3, 4))):
        near_is_own = place_of < 2
        half = lax.rem(place_of, 2)
        for out, row in zip(outs, (core, 1 - core)):

            def put(t, v):
                out[half, 0, t] = v

            def add(t, v):
                out[half, 0, t] = out[half, 0, t] + v

            at = (0, row) if by_core else (0,)
            stitch(
                lambda t: jnp.where(near_is_own, near[*at, t], far[*at, t]),
                lambda t: jnp.where(near_is_own, far[*at, t], near[*at, t]),
                put,
                add,
                shift,
            )


def stitch_pairs(parts, info, deps=()):
    count, by_core = parts[0].shape[0], parts[0].ndim == 5
    block = (1,) + parts[0].shape[1:]
    outs = [jax.ShapeDtypeStruct((2, count, CT, SUB, LANES), f32)] * (2 if by_core else 1)
    return pl.pallas_call(
        functools.partial(stitch_kernel, by_core),
        out_shape=outs + [TOKEN],
        in_specs=[SMEM]
        + [pl.BlockSpec(block, lambda o: (o,) + (0,) * (len(block) - 1))] * 4
        + [ANYWHERE] * len(deps),
        out_specs=[pl.BlockSpec((2, 1, CT, SUB, LANES), lambda o: (0, o, 0, 0, 0))] * len(outs) + [TOKEN_SPEC],
        grid=(count,),
        compiler_params=limit(8),
        cost_estimate=cost(1.5),
        name="stitch_pairs",
    )(info, *parts, *deps)


SLOTS = 5


def ramp_kernel(sources, info, *refs):
    rows, (tw_ref, gain_ref, fh, fl, gh, gl) = refs[:sources], refs[sources : sources + 6]
    out_ref, token, (sig, mid, spec) = refs[-5], refs[-4], refs[-3:]
    token[...] = jnp.zeros_like(token)
    steps = [(source, which) for source in rows for which in range(source.shape[1])]
    for n, (source, which) in enumerate(steps):

        @pl.when(pl.program_id(0) == n)
        def _():
            for half in range(2):
                place(lambda t: source[half, which, t], sig, half, info[1])

    def write(half, n, value):
        out_ref[half, 0, 0, 0, :, n * LANES : (n + 1) * LANES] = value

    ramp(sig, mid, spec, tw_ref, gain_ref, fh, fl, gh, gl, write)


def constants():
    twiddle, gain, forward = tables()
    fh, fl = split(forward)
    gh, gl = split(forward.T.copy())
    return [jnp.asarray(v) for v in (twiddle, gain, fh, fl, gh, gl)]


def ramp_filter(rows, info, consts, slot, result=None, deps=()):
    steps = sum(v.shape[1] for v in rows)
    local = pl.BlockSpec(memory_space=pltpu.VMEM)
    in_specs = [local] * (len(rows) + len(consts)) + [ANYWHERE] * len(deps)
    operands = [*rows, *consts, *deps]
    alias = {}
    if result is not None:
        alias = {1 + len(operands): 0}
        in_specs.append(ANYWHERE)
        operands.append(result)

    def target(i, info):
        at = SLOTS + 3 * (slot + i)
        return (0, info[at], info[at + 1], info[at + 2], 0, 0)

    return pl.pallas_call(
        functools.partial(ramp_kernel, len(rows)),
        out_shape=[jax.ShapeDtypeStruct((2, 2, 2, 2, SUB, S), f32), TOKEN],
        grid_spec=pltpu.PrefetchScalarGridSpec(
            num_scalar_prefetch=1,
            grid=(steps,),
            in_specs=in_specs,
            out_specs=[pl.BlockSpec((2, 1, 1, 1, SUB, S), target), whole((SUB, LANES))],
            scratch_shapes=[
                pltpu.VMEM((2, ST + 2, SUB, LANES), f32),
                pltpu.VMEM((2, 64, SUB, LANES), f32),
                pltpu.VMEM((64 * SUB, 2 * LANES), f32),
            ],
        ),
        input_output_aliases=alias,
        compiler_params=limit(16),
        cost_estimate=cost(2.0),
        name="ramp_filter",
    )(info, *operands)


def y_step(block, s):
    route = [(i, (i // 4 + s) % 4 * 4 + i % 4) for i in range(16)]
    return lax.ppermute(block, "ang", route)


def flip(block, bits):
    return lax.ppermute(block, "ang", [(i, i ^ bits) for i in range(16)])


def row_step(block, up_side):
    rows, angs = lax.axis_size("row"), lax.axis_size("ang")
    route = []
    for r in range(rows):
        for a in range(angs):
            to = r + 1 if a // 2 % 2 == up_side else r - 1
            if 0 <= to < rows:
                route.append((a * rows + r, a * rows + to))
    return lax.ppermute(block, ("ang", "row"), route)


def shards(projections, phase_kernel, correlation, offset):
    me = lax.axis_index("ang").astype(jnp.uint32)
    y, x, core = [v.astype(jnp.int32) for v in (me >> 2, (me >> 1) & 1, me & 1)]
    slots = []
    for x_of, core_of, octet in (
        (1 - x, core, 0),
        (1 - x, 1 - core, 0),
        (1 - x, core, 1),
        (1 - x, 1 - core, 1),
        (x, core, 0),
        (x, core, 1),
        (x, 1 - core, 0),
        (x, 1 - core, 1),
    ):
        slots += [x_of, core_of, jnp.int32(octet)]
    info = jnp.stack([correlation[0], offset[0], y, x, core] + slots)
    consts = constants()

    def y_exchange(parts):
        return [parts[0]] + [y_step(parts[s], s) for s in (1, 2, 3)]

    def send(rows):
        return flip(rows[0], 2), flip(rows[1], 3)

    edge = lax.dynamic_slice(projections, (0, 14 * x, 0), (16, 2, W))
    near = [row_step(jnp.swapaxes(edge, 0, 1), 1)] * 2
    xt = gather_rows(projections.reshape(256, W))
    xt, *sent_0, edges_0, done = phase_filter(xt, near[0], phase_kernel, info, 0, 1, True, [], (0, 1))
    far = row_step(edges_0, 0)
    parts_0 = y_exchange(sent_0)
    xt, *sent_1, edges_1, done = phase_filter(xt, near[1], phase_kernel, info, 1, 1, True, [done], ())
    parts_1 = y_exchange(sent_1)
    *rows_0, done = stitch_pairs(parts_0, info, [done])
    arrived_0 = send(rows_0)
    xt, *sent_2, _, done = phase_filter(xt, far, phase_kernel, info, 0, 2, False, [done])
    parts_2 = y_exchange(sent_2)
    *rows_1, done = stitch_pairs(parts_1, info, [done])
    arrived_1 = send(rows_1)
    result, done = ramp_filter([*arrived_0, arrived_1[0]], info, consts, 0, None, [done])
    *rows_2, done = stitch_pairs(parts_2, info, [done, arrived_1[0][0, 0, 0], arrived_1[1][0, 0, 0]])
    swapped = flip(rows_2[1], 1)
    result, done = ramp_filter([arrived_1[1], rows_2[0]], info, consts, 3, result)
    result, done = ramp_filter([swapped], info, consts, 6, result)
    return result.reshape(1, 128, S)


def solution(mesh):
    return jax.shard_map(
        shards,
        mesh=mesh,
        in_specs=(P("ang", "row", None), P(), P(), P()),
        out_specs=P(("row", "ang"), None, None),
        check_vma=False,
    )
```
